512 devices in a mesh: phase: 8 (over y, x_hi), blk: 64 (over x_lo, z, core).
Axes of the slice: x: 4 (x_hi: 2, x_lo: 2; x = x_hi * 2 + x_lo), y: 4, z: 16, core: 2. Of those that a mesh axis runs over, the one named last changes fastest.
Arguments:
- layer_input: bfloat16 [1024, 8192], P(None, 'blk'), may hold values from -40 to 40
- norm_gain: bfloat16 [8192], P('blk'), may hold values from 0.099609375 to 1.8984375
- gate_weight: bfloat16 [26624, 8192], P(('phase', 'blk')), may hold values from -0.0625 to 0.0625
- up_weight: bfloat16 [26624, 8192], P(('phase', 'blk')), may hold values from -0.0625 to 0.0625
- down_weight: bfloat16 [26624, 8192], P('phase', 'blk'), may hold values from -0.0390625 to 0.0390625
Outputs:
- layer_output: bfloat16 [1024, 8192], P('phase', 'blk')
The draws below stay inside these ranges and needn't reach their ends.
All inputs are finite; a program needn't handle non-finite values.
Results may differ from the reference program's by a relative error of at most 0.0056.
Values may be sent and summed in bfloat16 or wider, within the bound.
No kernel may reach another device: no remote copies, remote signals or barrier semaphores. Data moves between devices by JAX's collectives and lax.ppermute only.
A program may use at most 64 MiB of HBM per device.

```python
import math
import jax
import jax.numpy as jnp
from jax import lax

FEAT = 8192
FFN = 26624
ROWS = 1024


def draw_layer_input(key, part):
    key_rows, key_cols, key_base = jax.random.split(key, 3)
    ramp = 0.3 * jnp.exp(math.log(3.0) * jnp.arange(FEAT, dtype=jnp.float32) / FEAT)
    col_scale = ramp * jnp.exp(jax.random.uniform(key_cols, (1, FEAT), jnp.float32, math.log(0.5), math.log(2.0)))
    row_scale = jnp.exp(jax.random.uniform(key_rows, (ROWS, 1), jnp.float32, math.log(0.3), math.log(3.0)))
    base = jnp.clip(jax.random.normal(key_base, (ROWS, FEAT), jnp.float32), -6.0, 6.0)
    return (base * row_scale * col_scale).astype(jnp.bfloat16)


def block_scale(own_key, extent, cuts, smallest, top_value):
    level, own = 1.0, jax.random.fold_in(own_key, 6)
    for dim, shards_of in cuts:
        draws = jnp.exp(jax.random.uniform(jax.random.fold_in(own, dim), (shards_of,), jnp.float32, smallest / len(cuts), top_value / len(cuts)))
        level = level * jnp.repeat(draws, extent[dim] // shards_of).reshape([-1 if axis == dim else 1 for axis in range(len(extent))])
    return level


def scatter_about(stream_key, shape, width, bound, cuts=(), kind=jnp.bfloat16):
    gain = block_scale(stream_key, shape, cuts, -0.22, 0.18) if cuts else 1.0
    result = jax.random.normal(stream_key, shape, jnp.float32) * width * gain
    return jnp.minimum(jnp.maximum(result, -bound), bound).astype(kind)


def setup_inputs(seed: int = 0) -> dict:
    keys = jax.random.split(jax.random.key(seed), 6)
    return {
        "layer_input": draw_layer_input(jax.random.fold_in(keys[5], 71), 0),
        "norm_gain": jnp.clip(1.0 + 0.18 * jax.random.normal(keys[1], (FEAT,), jnp.float32), 0.099609375, 1.8984375).astype(jnp.bfloat16),
        "gate_weight": scatter_about(keys[2], (FFN, FEAT), FEAT ** -0.5, 0.0625, ((0, 512),)),
        "up_weight": scatter_about(keys[3], (FFN, FEAT), FEAT ** -0.5, 0.0625, ((0, 512),)),
        "down_weight": scatter_about(keys[4], (FFN, FEAT), FFN ** -0.5, 0.0390625, ((0, 8), (1, 64))),
    }


epsilon = 1e-05

def times_rows(left, weight):
    return lax.dot_general(left, weight, (((1,), (1,)), ((), ())), preferred_element_type=jnp.float32)

def reference(layer_input, norm_gain, gate_weight, up_weight, down_weight):
    widened = layer_input.astype(jnp.float32)
    inv_rms = lax.rsqrt(lax.optimization_barrier(jnp.mean(widened * widened, axis=1, keepdims=True)) + epsilon)
    normed = (widened * inv_rms * norm_gain.astype(jnp.float32)).astype(jnp.bfloat16)
    gate_sum = times_rows(normed, gate_weight)
    up_sum = times_rows(normed, up_weight)
    activated = (jax.nn.silu(gate_sum) * up_sum).astype(jnp.bfloat16)
    ffn_out = jnp.dot(activated, down_weight, preferred_element_type=jnp.float32)
    return (widened + ffn_out).astype(jnp.bfloat16)
```

```python
import jax
import jax.numpy as jnp
from jax import lax
from jax.sharding import Mesh, PartitionSpec as P

FEAT = 8192
EPS = 1e-05
LANES = 128

AXES = ("y", "xh", "xl", "zh", "zm", "z0", "core")
SIZES = (4, 2, 2, 4, 2, 2, 2)
PHASE = ("y", "xh")
BLK = ("xl", "zh", "zm", "z0", "core")
GROUP = ("zh", "zm")
MEMBER = ("xl", "z0")
NEAR = ("xl", "zm", "z0")
FAR = "zh"

f32, bf16 = jnp.float32, jnp.bfloat16


def swap_cores(value):
    return lax.ppermute(value, "core", ((0, 1), (1, 0)))


def exchange(value, axes):
    return lax.all_to_all(value, axes, 0, 0, tiled=True)


def copies(value, count):
    return jnp.broadcast_to(value[None], (count, *value.shape))


def by_core(own, other, axis):
    first = lax.axis_index("core") == 0
    return jnp.stack((jnp.where(first, own, other), jnp.where(first, other, own)), axis)


def local(layer_input, norm_gain, gate_weight, up_weight, down_weight):
    phase = lax.axis_index(PHASE)
    units = gate_weight.shape[0]
    rows = layer_input.shape[0] // 16

    both = jnp.concatenate((gate_weight, up_weight), 0)
    both = both.reshape(2 * units, 2, 8, 512).transpose(2, 0, 1, 3)
    own_w = exchange(both.reshape(8, 2 * units, 1024), PHASE)
    other_w = swap_cores(own_w)
    down = down_weight.reshape(2, 4, 8 * units, LANES).transpose(1, 0, 2, 3)
    down = exchange(down.reshape(4, 16 * units, LANES), FAR)
    other_down = swap_cores(down)

    mine = lax.dynamic_slice_in_dim(layer_input, phase * 2 * rows, 2 * rows, 0)
    gain = jnp.broadcast_to(norm_gain[None, None], (2, 8, LANES))
    mine = jnp.concatenate((mine.reshape(2, rows, LANES), gain), 1)
    sent = jnp.broadcast_to(mine[None], (8, 2, rows + 8, LANES))
    got = exchange(sent.reshape(16, rows + 8, LANES), (*GROUP, "core"))
    got = exchange(got.reshape(8, 2, rows + 8, LANES), PHASE)
    got = exchange(copies(got, 4), MEMBER)
    gains = got[:, :1, :, rows : rows + 1].astype(f32)
    vals = got[:, :, :, :rows].astype(f32)
    sq = jnp.sum(vals * vals, axis=(0, 2, 4)).reshape(8 * rows)
    scaled = (vals * gains).astype(bf16).transpose(1, 3, 0, 2, 4).reshape(8 * rows, 1024)

    def times(weight):
        return lax.dot_general(
            weight.reshape(16 * units, 1024),
            scaled,
            (((1,), (1,)), ((), ())),
            preferred_element_type=f32,
        ).astype(bf16).reshape(8, 2 * units, 8 * rows)

    sq_hi = sq.astype(bf16)
    sq_rest = sq - sq_hi.astype(f32)
    sq_mid = sq_rest.astype(bf16)
    sq_lo = (sq_rest - sq_mid.astype(f32)).astype(bf16)
    zero = jnp.zeros_like(sq_hi)
    sq_rows = jnp.stack((sq_hi, sq_mid, sq_lo, zero, zero, zero, zero, zero))
    sums = jnp.concatenate((times(own_w), times(other_w), copies(sq_rows, 8)), 1)
    sums = jnp.sum(exchange(sums, PHASE).astype(f32), 0)
    sq_total = jnp.sum(sums[4 * units : 4 * units + 3], 0)
    inv_rms = lax.rsqrt(sq_total / FEAT + EPS)
    sums = sums[: 4 * units].reshape(2, 2, units, 8 * rows) * inv_rms
    acts = (jax.nn.silu(sums[:, 0]) * sums[:, 1]).astype(bf16)
    acts = by_core(acts[0], acts[1], 0).reshape(2 * units, 8 * rows)

    acts = exchange(copies(acts, 8), NEAR).reshape(16 * units, 8 * rows)
    weights = by_core(down, other_down, 1).transpose(2, 0, 1, 3).reshape(16 * units, 1024)
    partials = lax.dot_general(
        acts, weights, (((0,), (0,)), ((), ())), preferred_element_type=f32
    ).astype(bf16)
    partials = exchange(partials.reshape(8, rows, 1024), PHASE)
    partials = jnp.sum(partials.astype(f32), 0).astype(bf16)
    partials = partials.reshape(rows, 8, LANES).transpose(1, 0, 2)
    partials = exchange(partials, (FAR, "core")).astype(f32)
    ffn_out = jnp.sum(partials.reshape(4, 2 * rows, LANES), 0)
    residual = lax.dynamic_slice_in_dim(layer_input, phase * 2 * rows, 2 * rows, 0)
    return (residual.astype(f32) + ffn_out).astype(bf16)


def solution(mesh):
    fine = Mesh(mesh.devices.reshape(SIZES), AXES)
    return jax.shard_map(
        local,
        mesh=fine,
        in_specs=(
            P(None, BLK),
            P(BLK),
            P((*PHASE, *BLK), None),
            P((*PHASE, *BLK), None),
            P(PHASE, BLK),
        ),
        out_specs=P(PHASE, BLK),
        check_vma=False,
    )
```

```python
import jax
import jax.numpy as jnp
import numpy as np
from jax import lax
from jax.experimental import pallas as pl
from jax.experimental.pallas import tpu as pltpu
from jax.sharding import Mesh, PartitionSpec as P

FEAT = 8192
EPS = 1e-05
LANES = 128
PAD = 16

AXES = ("y", "xh", "xl", "zh", "zm", "z0", "core")
SIZES = (4, 2, 2, 4, 2, 2, 2)
PHASE = ("y", "xh")
BLK = ("xl", "zh", "zm", "z0", "core")
NEAR = ("xl", "zm", "z0")
FAR = "zh"

f32, bf16 = jnp.float32, jnp.bfloat16


def exchange(value, axes):
    return lax.all_to_all(value, axes, 0, 0, tiled=True)


def route(move):
    pairs = []
    for at in np.ndindex(*SIZES):
        to = dict(zip(AXES, at))
        move(to)
        to = tuple(to[a] % n for a, n in zip(AXES, SIZES))
        pairs.append([int(np.ravel_multi_index(i, SIZES)) for i in (at, to)])
    return pairs


def send(value, move):
    return lax.ppermute(value, AXES, route(move))


def spread(turn, cross):
    def move(to):
        part, group = to["y"] * 2 + to["xh"], to["zh"] * 2 + to["zm"]
        to["y"], to["xh"] = divmod(group, 2)
        to["zh"], to["zm"] = divmod((part + turn - group) % 8, 2)
        to["core"] += cross

    return move


def shift(**by):
    def move(to):
        for axis, count in by.items():
            to[axis] += count

    return move


def sums_kernel(at, x0, x1, x2, x3, w_own, w_other, out, scaled):
    rows = scaled.shape[0]
    squares = jnp.zeros((rows, LANES), f32)
    for chip, block in enumerate((x0, x1, x2, x3)):
        for core in (0, 1):
            vals = block[core, :rows].astype(f32)
            gain = block[core, rows:].astype(f32)[:1]
            squares += vals * vals
            place = (jnp.bitwise_xor(at[1], chip) * 2 + jnp.bitwise_xor(at[0], core)) * LANES
            scaled[:, pl.ds(pl.multiple_of(place, LANES), LANES)] = (vals * gain).astype(bf16)
    total = lax.dot_general(
        jnp.ones((8, LANES), f32),
        squares,
        (((1,), (1,)), ((), ())),
        precision=lax.Precision.HIGHEST,
        preferred_element_type=f32,
    )
    hi = total.astype(bf16).astype(f32)
    mid = (total - hi).astype(bf16).astype(f32)
    row = lax.broadcasted_iota(jnp.int32, (8, rows), 0)
    extra = jnp.where(row == 4, hi, jnp.where(row == 5, mid, jnp.where(row == 6, total - hi - mid, 0.0)))
    extra = jnp.concatenate((jnp.zeros((48, rows), f32), extra, jnp.zeros((56, rows), f32)))
    right = scaled[...]
    for side, weight in enumerate((w_own, w_other)):
        part = lax.dot_general(
            weight[...].reshape(8 * 112, 1024),
            right,
            (((1,), (1,)), ((), ())),
            preferred_element_type=f32,
        ).reshape(8, 112, rows)
        if side == 0:
            part = part + extra[None]
        out[:, side] = part.astype(bf16)


def acts_kernel(at, sums, out):
    rows = sums.shape[-1]
    own = sums[0, 0].astype(f32)
    other = sums[0, 1].astype(f32)
    for part in range(1, 8):
        own += sums[part, 0].astype(f32)
        other += sums[part, 1].astype(f32)
    row = lax.broadcasted_iota(jnp.int32, (8, rows), 0)
    squares = jnp.where((row >= 4) & (row < 7), own[48:56], 0.0)
    inv_rms = lax.rsqrt(jnp.sum(squares, 0, keepdims=True) / FEAT + EPS)
    unit = lax.broadcasted_iota(jnp.int32, (56, rows), 0)
    for side, total in enumerate((own, other)):
        gate = total[:56] * inv_rms
        acts = gate / (1.0 + jnp.exp(-gate)) * (total[56:] * inv_rms)
        acts = jnp.where(unit < 52, acts, 0.0).astype(bf16)
        for copy in range(8):
            out[copy, jnp.bitwise_xor(at[0], side)] = acts


def place_kernel(at, parts, out):
    total = parts[0].astype(f32)
    for part in range(1, 8):
        total += parts[part].astype(f32)
    for far in range(4):
        for core in (0, 1):
            to = jnp.bitwise_and(at[2] - far, 3) * 2 + jnp.bitwise_xor(at[0], core)
            column = (far * 2 + core) * LANES
            out[to] = total[:, column : column + LANES].astype(bf16)


def run(kernel, out_shape, operands, scratch=(), flops=0):
    moved = sum(o.size * o.dtype.itemsize for o in operands) + int(np.prod(out_shape)) * 2
    return pl.pallas_call(
        kernel,
        out_shape=jax.ShapeDtypeStruct(out_shape, bf16),
        in_specs=[pl.BlockSpec(memory_space=pltpu.SMEM)]
        + [pl.BlockSpec(memory_space=pltpu.VMEM)] * (len(operands) - 1),
        out_specs=pl.BlockSpec(memory_space=pltpu.VMEM),
        scratch_shapes=list(scratch),
        compiler_params=pltpu.CompilerParams(vmem_limit_bytes=40 * 2**20),
        cost_estimate=pl.CostEstimate(flops=flops, bytes_accessed=moved, transcendentals=0),
    )(*operands)


def local(layer_input, norm_gain, gate_weight, up_weight, down_weight):
    phase, core, far = (lax.axis_index(a) for a in (PHASE, "core", FAR))
    at = jnp.stack((core, lax.axis_index(("xl", "z0")), far)).astype(jnp.int32)
    units = gate_weight.shape[0]
    rows = layer_input.shape[0] // 2

    halves = layer_input.reshape(8, 2, rows // 8, LANES)
    gain = jnp.broadcast_to(norm_gain[None], (PAD, LANES))

    def half(index):
        part = lax.dynamic_slice_in_dim(halves, index, 1, 1).reshape(rows, LANES)
        return jnp.concatenate((part, gain))

    mine, yours, gate_weight, up_weight = lax.optimization_barrier(
        (half(core), half(1 - core), gate_weight, up_weight)
    )
    both = jnp.stack((gate_weight, up_weight))
    both = jnp.pad(both, ((0, 0), (0, 56 - units), (0, 0))).reshape(112, 2, 8, 512)
    own_w = exchange(both.transpose(2, 0, 1, 3).reshape(8, 112, 1024), PHASE)
    first = send(mine, spread(0, 0))
    second = send(yours, spread(4, 1))
    first, second, own_w = lax.optimization_barrier((first, second, own_w))
    other_w = send(own_w, shift(core=1))
    held = jnp.stack((first, second))
    blocks = [held] + [send(held, shift(xl=i, z0=j)) for i, j in ((0, 1), (1, 0), (1, 1))]

    down, _ = lax.optimization_barrier((down_weight, held))
    down = down.reshape(2, 4, 8, units, LANES)
    down = jnp.pad(down, ((0, 0), (0, 0), (0, 0), (0, 56 - units), (0, 0)))

    def quarter(count):
        part = lax.dynamic_slice_in_dim(down, (far + count) % 4, 1, 1).reshape(896, LANES)
        return send(part, shift(zh=count)) if count else part

    own_d = jnp.stack([quarter(count) for count in range(4)])
    sums = run(
        sums_kernel,
        (8, 2, 112, rows),
        (at, *blocks, own_w, other_w),
        (pltpu.VMEM((rows, 1024), bf16),),
        flops=2 * 1792 * 1024 * rows,
    )
    sums, own_d = lax.optimization_barrier((exchange(sums, PHASE), own_d))
    other_d = send(own_d, shift(core=1))
    d_all = jnp.stack((own_d, other_d), 1).transpose(2, 0, 1, 3).reshape(896, 1024)

    acts = run(acts_kernel, (8, 2, 56, rows), (at, sums))
    acts = exchange(acts.reshape(8, 112, rows), NEAR).reshape(896, rows)
    partials = lax.dot_general(
        acts, d_all, (((0,), (0,)), ((), ())), preferred_element_type=f32
    ).astype(bf16)
    partials = exchange(partials.reshape(8, rows // 8, 1024), PHASE)
    partials = run(place_kernel, (8, rows // 8, LANES), (at, partials))
    partials = exchange(partials, (FAR, "core")).astype(f32)
    ffn_out = jnp.sum(partials.reshape(4, rows // 4, LANES), 0)
    residual = lax.dynamic_slice_in_dim(layer_input, phase * (rows // 4), rows // 4, 0)
    return (residual.astype(f32) + ffn_out).astype(bf16)


def solution(mesh):
    fine = Mesh(mesh.devices.reshape(SIZES), AXES)
    return jax.shard_map(
        local,
        mesh=fine,
        in_specs=(
            P(None, BLK),
            P(BLK),
            P((*PHASE, *BLK), None),
            P((*PHASE, *BLK), None),
            P(PHASE, BLK),
        ),
        out_specs=P(PHASE, BLK),
        check_vma=False,
    )
```

```python
import jax
import jax.numpy as jnp
import numpy as np
from jax import lax
from jax.experimental import pallas as pl
from jax.experimental.pallas import tpu as pltpu
from jax.sharding import Mesh, PartitionSpec as P

FEAT = 8192
EPS = 1e-05
LANES = 128
PAD = 16

AXES = ("y", "xh", "xl", "zh", "zm", "z0", "core")
SIZES = (4, 2, 2, 4, 2, 2, 2)
PHASE = ("y", "xh")
BLK = ("xl", "zh", "zm", "z0", "core")
NEAR = ("xl", "zm", "z0")
FAR = "zh"

f32, bf16 = jnp.float32, jnp.bfloat16


def exchange(value, axes):
    return lax.all_to_all(value, axes, 0, 0, tiled=True)


def route(move):
    pairs = []
    for at in np.ndindex(*SIZES):
        to = dict(zip(AXES, at))
        move(to)
        to = tuple(to[a] % n for a, n in zip(AXES, SIZES))
        pairs.append([int(np.ravel_multi_index(i, SIZES)) for i in (at, to)])
    return pairs


def send(value, move):
    return lax.ppermute(value, AXES, route(move))


def spread(turn, cross):
    def move(to):
        part, group = to["y"] * 2 + to["xh"], to["zh"] * 2 + to["zm"]
        to["y"], to["xh"] = divmod(group, 2)
        to["zh"], to["zm"] = divmod((part + turn - group) % 8, 2)
        to["core"] += cross

    return move


def shift(**by):
    def move(to):
        for axis, count in by.items():
            to[axis] += count

    return move


def sums_kernel(at, x0, x1, x2, x3, w_own, w_other, out, scaled):
    rows = scaled.shape[0]
    squares = jnp.zeros((rows, LANES), f32)
    for chip, block in enumerate((x0, x1, x2, x3)):
        for core in (0, 1):
            vals = block[core, :rows].astype(f32)
            gain = block[core, rows:].astype(f32)[:1]
            squares += vals * vals
            place = (jnp.bitwise_xor(at[1], chip) * 2 + jnp.bitwise_xor(at[0], core)) * LANES
            scaled[:, pl.ds(pl.multiple_of(place, LANES), LANES)] = (vals * gain).astype(bf16)
    total = lax.dot_general(
        jnp.ones((8, LANES), f32),
        squares,
        (((1,), (1,)), ((), ())),
        precision=lax.Precision.HIGHEST,
        preferred_element_type=f32,
    )
    hi = total.astype(bf16).astype(f32)
    mid = (total - hi).astype(bf16).astype(f32)
    row = lax.broadcasted_iota(jnp.int32, (8, rows), 0)
    extra = jnp.where(row == 4, hi, jnp.where(row == 5, mid, jnp.where(row == 6, total - hi - mid, 0.0)))
    extra = jnp.concatenate((jnp.zeros((48, rows), f32), extra, jnp.zeros((56, rows), f32)))
    right = scaled[...]
    for side, weight in enumerate((w_own, w_other)):
        part = lax.dot_general(
            weight[...].reshape(8 * 112, 1024),
            right,
            (((1,), (1,)), ((), ())),
            preferred_element_type=f32,
        ).reshape(8, 112, rows)
        if side == 0:
            part = part + extra[None]
        out[:, side] = part.astype(bf16)


def acts_kernel(at, sums, out):
    rows = sums.shape[-1]
    own = sums[0, 0].astype(f32)
    other = sums[0, 1].astype(f32)
    for part in range(1, 8):
        own += sums[part, 0].astype(f32)
        other += sums[part, 1].astype(f32)
    row = lax.broadcasted_iota(jnp.int32, (8, rows), 0)
    squares = jnp.where((row >= 4) & (row < 7), own[48:56], 0.0)
    inv_rms = lax.rsqrt(jnp.sum(squares, 0, keepdims=True) / FEAT + EPS)
    unit = lax.broadcasted_iota(jnp.int32, (56, rows), 0)
    for side, total in enumerate((own, other)):
        gate = total[:56] * inv_rms
        acts = gate / (1.0 + jnp.exp(-gate)) * (total[56:] * inv_rms)
        acts = jnp.where(unit < 52, acts, 0.0).astype(bf16)
        for copy in range(8):
            out[copy, jnp.bitwise_xor(at[0], side)] = acts


def place_kernel(at, parts, out):
    total = parts[0].astype(f32)
    for part in range(1, 8):
        total += parts[part].astype(f32)
    for far in range(4):
        for core in (0, 1):
            to = jnp.bitwise_and(at[2] - far, 3) * 2 + jnp.bitwise_xor(at[0], core)
            column = (far * 2 + core) * LANES
            out[to] = total[:, column : column + LANES].astype(bf16)


def run(kernel, out_shape, operands, scratch=(), flops=0):
    moved = sum(o.size * o.dtype.itemsize for o in operands) + int(np.prod(out_shape)) * 2
    return pl.pallas_call(
        kernel,
        out_shape=jax.ShapeDtypeStruct(out_shape, bf16),
        in_specs=[pl.BlockSpec(memory_space=pltpu.SMEM)]
        + [pl.BlockSpec(memory_space=pltpu.VMEM)] * (len(operands) - 1),
        out_specs=pl.BlockSpec(memory_space=pltpu.VMEM),
        scratch_shapes=list(scratch),
        compiler_params=pltpu.CompilerParams(vmem_limit_bytes=40 * 2**20),
        cost_estimate=pl.CostEstimate(flops=flops, bytes_accessed=moved, transcendentals=0),
    )(*operands)


def local(layer_input, norm_gain, gate_weight, up_weight, down_weight):
    phase, core, far = (lax.axis_index(a) for a in (PHASE, "core", FAR))
    at = jnp.stack((core, lax.axis_index(("xl", "z0")), far)).astype(jnp.int32)
    units = gate_weight.shape[0]
    rows = layer_input.shape[0] // 2

    halves = layer_input.reshape(8, 2, rows // 8, LANES)
    gain = jnp.broadcast_to(norm_gain[None], (PAD, LANES))

    def half(index):
        part = lax.dynamic_slice_in_dim(halves, index, 1, 1).reshape(rows, LANES)
        return jnp.concatenate((part, gain))

    mine, yours, gate_weight, up_weight = lax.optimization_barrier(
        (half(core), half(1 - core), gate_weight, up_weight)
    )
    first = send(mine, spread(0, 0))
    second = send(yours, spread(4, 1))
    both = jnp.stack((gate_weight, up_weight))
    both = jnp.pad(both, ((0, 0), (0, 56 - units), (0, 0))).reshape(112, 2, 8, 512)
    both = both.transpose(2, 0, 1, 3).reshape(8, 112, 1024)
    first, second, both = lax.optimization_barrier((first, second, both))
    own_w = exchange(both, PHASE)
    held = jnp.stack((first, second))
    blocks = [held] + [send(held, shift(xl=i, z0=j)) for i, j in ((0, 1), (1, 0), (1, 1))]
    *blocks, own_w = lax.optimization_barrier((*blocks, own_w))
    other_w = send(own_w, shift(core=1))

    down, _ = lax.optimization_barrier((down_weight, held))
    down = down.reshape(2, 4, 8, units, LANES)
    down = jnp.pad(down, ((0, 0), (0, 0), (0, 0), (0, 56 - units), (0, 0)))

    def quarter(count):
        part = lax.dynamic_slice_in_dim(down, (far + count) % 4, 1, 1).reshape(896, LANES)
        return send(part, shift(zh=count)) if count else part

    quarters = [quarter(count) for count in range(4)]
    sums = run(
        sums_kernel,
        (8, 2, 112, rows),
        (at, *blocks, own_w, other_w),
        (pltpu.VMEM((rows, 1024), bf16),),
        flops=2 * 1792 * 1024 * rows,
    )
    sums, quarters[1], quarters[3] = lax.optimization_barrier((sums, quarters[1], quarters[3]))
    sums, quarters[2] = lax.optimization_barrier((exchange(sums, PHASE), quarters[2]))
    own_d = jnp.stack(quarters)
    other_d = send(own_d, shift(core=1))
    d_all = jnp.stack((own_d, other_d), 1).transpose(2, 0, 1, 3).reshape(896, 1024)

    acts = run(acts_kernel, (8, 2, 56, rows), (at, sums))
    acts = exchange(acts.reshape(8, 112, rows), NEAR).reshape(896, rows)
    partials = lax.dot_general(
        acts, d_all, (((0,), (0,)), ((), ())), preferred_element_type=f32
    ).astype(bf16)
    partials = exchange(partials.reshape(8, rows // 8, 1024), PHASE)
    partials = run(place_kernel, (8, rows // 8, LANES), (at, partials))
    partials = exchange(partials, (FAR, "core")).astype(f32)
    ffn_out = jnp.sum(partials.reshape(4, rows // 4, LANES), 0)
    residual = lax.dynamic_slice_in_dim(layer_input, phase * (rows // 4), rows // 4, 0)
    return (residual.astype(f32) + ffn_out).astype(bf16)


def solution(mesh):
    fine = Mesh(mesh.devices.reshape(SIZES), AXES)
    return jax.shard_map(
        local,
        mesh=fine,
        in_specs=(
            P(None, BLK),
            P(BLK),
            P((*PHASE, *BLK), None),
            P((*PHASE, *BLK), None),
            P(PHASE, BLK),
        ),
        out_specs=P(PHASE, BLK),
        check_vma=False,
    )
```

```python
import jax
import jax.numpy as jnp
import numpy as np
from jax import lax
from jax.experimental import pallas as pl
from jax.experimental.pallas import tpu as pltpu
from jax.sharding import Mesh, PartitionSpec as P

FEAT = 8192
EPS = 1e-05
LANES = 128
PAD = 16

AXES = ("y", "xh", "xl", "zh", "zm", "z0", "core")
SIZES = (4, 2, 2, 4, 2, 2, 2)
PHASE = ("y", "xh")
BLK = ("xl", "zh", "zm", "z0", "core")
NEAR = ("xl", "zm", "z0")
FAR = "zh"

f32, bf16 = jnp.float32, jnp.bfloat16


def exchange(value, axes):
    return lax.all_to_all(value, axes, 0, 0, tiled=True)


def route(move):
    pairs = []
    for at in np.ndindex(*SIZES):
        to = dict(zip(AXES, at))
        move(to)
        to = tuple(to[a] % n for a, n in zip(AXES, SIZES))
        pairs.append([int(np.ravel_multi_index(i, SIZES)) for i in (at, to)])
    return pairs


def send(value, move):
    return lax.ppermute(value, AXES, route(move))


def spread(turn, cross):
    def move(to):
        part, group = to["y"] * 2 + to["xh"], to["zh"] * 2 + to["zm"]
        to["y"], to["xh"] = divmod(group, 2)
        to["zh"], to["zm"] = divmod((part + turn - group) % 8, 2)
        to["core"] += cross

    return move


def shift(**by):
    def move(to):
        for axis, count in by.items():
            to[axis] += count

    return move


def cut_kernel(at, both, out):
    del at
    for group in range(8):
        for side in (0, 1):
            start = side * FEAT // 2 + group * 512
            out[group, :, side * 512 : side * 512 + 512] = both[:, start : start + 512]


def sums_kernel(at, x0, x1, x2, x3, w_own, w_other, out, scaled):
    rows = scaled.shape[0]
    squares = jnp.zeros((rows, LANES), f32)
    for chip, block in enumerate((x0, x1, x2, x3)):
        for core in (0, 1):
            vals = block[core, :rows].astype(f32)
            gain = block[core, rows:].astype(f32)[:1]
            squares += vals * vals
            place = (jnp.bitwise_xor(at[1], chip) * 2 + jnp.bitwise_xor(at[0], core)) * LANES
            scaled[:, pl.ds(pl.multiple_of(place, LANES), LANES)] = (vals * gain).astype(bf16)
    total = lax.dot_general(
        jnp.ones((8, LANES), f32),
        squares,
        (((1,), (1,)), ((), ())),
        precision=lax.Precision.HIGHEST,
        preferred_element_type=f32,
    )
    hi = total.astype(bf16).astype(f32)
    mid = (total - hi).astype(bf16).astype(f32)
    row = lax.broadcasted_iota(jnp.int32, (8, rows), 0)
    extra = jnp.where(row == 4, hi, jnp.where(row == 5, mid, jnp.where(row == 6, total - hi - mid, 0.0)))
    extra = jnp.concatenate((jnp.zeros((48, rows), f32), extra, jnp.zeros((56, rows), f32)))
    right = scaled[...]
    for side, weight in enumerate((w_own, w_other)):
        part = lax.dot_general(
            weight[...].reshape(8 * 112, 1024),
            right,
            (((1,), (1,)), ((), ())),
            preferred_element_type=f32,
        ).reshape(8, 112, rows)
        if side == 0:
            part = part + extra[None]
        out[:, side] = part.astype(bf16)


def acts_kernel(at, sums, out):
    rows = sums.shape[-1]
    own = sums[0, 0].astype(f32)
    other = sums[0, 1].astype(f32)
    for part in range(1, 8):
        own += sums[part, 0].astype(f32)
        other += sums[part, 1].astype(f32)
    row = lax.broadcasted_iota(jnp.int32, (8, rows), 0)
    squares = jnp.where((row >= 4) & (row < 7), own[48:56], 0.0)
    inv_rms = lax.rsqrt(jnp.sum(squares, 0, keepdims=True) / FEAT + EPS)
    unit = lax.broadcasted_iota(jnp.int32, (56, rows), 0)
    for side, total in enumerate((own, other)):
        gate = total[:56] * inv_rms
        acts = gate / (1.0 + jnp.exp(-gate)) * (total[56:] * inv_rms)
        acts = jnp.where(unit < 52, acts, 0.0).astype(bf16)
        for copy in range(8):
            out[copy, jnp.bitwise_xor(at[0], side)] = acts


def place_kernel(at, parts, out):
    total = parts[0].astype(f32)
    for part in range(1, 8):
        total += parts[part].astype(f32)
    for far in range(4):
        for core in (0, 1):
            to = jnp.bitwise_and(at[2] - far, 3) * 2 + jnp.bitwise_xor(at[0], core)
            column = (far * 2 + core) * LANES
            out[to] = total[:, column : column + LANES].astype(bf16)


def run(kernel, out_shape, operands, scratch=(), flops=0):
    moved = sum(o.size * o.dtype.itemsize for o in operands) + int(np.prod(out_shape)) * 2
    return pl.pallas_call(
        kernel,
        out_shape=jax.ShapeDtypeStruct(out_shape, bf16),
        in_specs=[pl.BlockSpec(memory_space=pltpu.SMEM)]
        + [pl.BlockSpec(memory_space=pltpu.VMEM)] * (len(operands) - 1),
        out_specs=pl.BlockSpec(memory_space=pltpu.VMEM),
        scratch_shapes=list(scratch),
        compiler_params=pltpu.CompilerParams(vmem_limit_bytes=40 * 2**20),
        cost_estimate=pl.CostEstimate(flops=flops, bytes_accessed=moved, transcendentals=0),
    )(*operands)


def local(layer_input, norm_gain, gate_weight, up_weight, down_weight):
    phase, core, far = (lax.axis_index(a) for a in (PHASE, "core", FAR))
    at = jnp.stack((core, lax.axis_index(("xl", "z0")), far)).astype(jnp.int32)
    units = gate_weight.shape[0]
    rows = layer_input.shape[0] // 2

    halves = layer_input.reshape(8, 2, rows // 8, LANES)
    gain = jnp.broadcast_to(norm_gain[None], (PAD, LANES))

    def half(index):
        part = lax.dynamic_slice_in_dim(halves, index, 1, 1).reshape(rows, LANES)
        return jnp.concatenate((part, gain))

    both = jnp.stack((gate_weight, up_weight))
    both = jnp.pad(both, ((0, 0), (0, 56 - units), (0, 0))).reshape(112, FEAT)
    own_w = exchange(run(cut_kernel, (8, 112, 1024), (at, both)), PHASE)
    first = send(half(core), spread(0, 0))
    second = send(half(1 - core), spread(4, 1))
    first, second, own_w = lax.optimization_barrier((first, second, own_w))
    other_w = send(own_w, shift(core=1))
    held = jnp.stack((first, second))
    blocks = [held] + [send(held, shift(xl=i, z0=j)) for i, j in ((0, 1), (1, 0), (1, 1))]

    down, _ = lax.optimization_barrier((down_weight, held))
    down = down.reshape(2, 4, 8, units, LANES)
    down = jnp.pad(down, ((0, 0), (0, 0), (0, 0), (0, 56 - units), (0, 0)))

    def quarter(count):
        part = lax.dynamic_slice_in_dim(down, (far + count) % 4, 1, 1).reshape(896, LANES)
        return send(part, shift(zh=count)) if count else part

    quarters = [quarter(count) for count in range(4)]
    sums = run(
        sums_kernel,
        (8, 2, 112, rows),
        (at, *blocks, own_w, other_w),
        (pltpu.VMEM((rows, 1024), bf16),),
        flops=2 * 1792 * 1024 * rows,
    )
    sums, quarters[1], quarters[3] = lax.optimization_barrier(
        (exchange(sums, PHASE), quarters[1], quarters[3])
    )
    own_d = jnp.stack(quarters)
    other_d = send(own_d, shift(core=1))
    d_all = jnp.stack((own_d, other_d), 1).transpose(2, 0, 1, 3).reshape(896, 1024)

    acts = run(acts_kernel, (8, 2, 56, rows), (at, sums))
    acts = exchange(acts.reshape(8, 112, rows), NEAR).reshape(896, rows)
    partials = lax.dot_general(
        acts, d_all, (((0,), (0,)), ((), ())), preferred_element_type=f32
    ).astype(bf16)
    partials = exchange(partials.reshape(8, rows // 8, 1024), PHASE)
    partials = run(place_kernel, (8, rows // 8, LANES), (at, partials))
    partials = exchange(partials, (FAR, "core")).astype(f32)
    ffn_out = jnp.sum(partials.reshape(4, rows // 4, LANES), 0)
    residual = lax.dynamic_slice_in_dim(layer_input, phase * (rows // 4), rows // 4, 0)
    return (residual.astype(f32) + ffn_out).astype(bf16)


def solution(mesh):
    fine = Mesh(mesh.devices.reshape(SIZES), AXES)
    return jax.shard_map(
        local,
        mesh=fine,
        in_specs=(
            P(None, BLK),
            P(BLK),
            P((*PHASE, *BLK), None),
            P((*PHASE, *BLK), None),
            P(PHASE, BLK),
        ),
        out_specs=P(PHASE, BLK),
        check_vma=False,
    )
```

```python
import jax
import jax.numpy as jnp
import numpy as np
from jax import lax
from jax.experimental import pallas as pl
from jax.experimental.pallas import tpu as pltpu
from jax.sharding import Mesh, PartitionSpec as P

FEAT = 8192
EPS = 1e-05
LANES = 128
PAD = 16

AXES = ("y", "xh", "xl", "zh", "zm", "z0", "core")
SIZES = (4, 2, 2, 4, 2, 2, 2)
PHASE = ("y", "xh")
BLK = ("xl", "zh", "zm", "z0", "core")
FAR = "zh"
BLOCK = ("xl", "zm", "z0")

f32, bf16 = jnp.float32, jnp.bfloat16


def exchange(value, axes):
    return lax.all_to_all(value, axes, 0, 0, tiled=True)


def route(move):
    pairs = []
    for at in np.ndindex(*SIZES):
        to = dict(zip(AXES, at))
        move(to)
        to = tuple(to[a] % n for a, n in zip(AXES, SIZES))
        pairs.append([int(np.ravel_multi_index(i, SIZES)) for i in (at, to)])
    return pairs


def send(value, move):
    return lax.ppermute(value, AXES, route(move))


def spread(turn, cross):
    def move(to):
        part, group = to["y"] * 2 + to["xh"], to["zh"] * 2 + to["zm"]
        to["y"], to["xh"] = divmod(group, 2)
        to["zh"], to["zm"] = divmod((part + turn - group) % 8, 2)
        to["core"] += cross

    return move


def shift(**by):
    def move(to):
        for axis, count in by.items():
            to[axis] += count

    return move


def cut_kernel(at, both, out):
    del at
    for group in range(8):
        for side in (0, 1):
            start = side * FEAT // 2 + group * 512
            out[group, :, side * 512 : side * 512 + 512] = both[:, start : start + 512]


def sums_kernel(at, x0, x1, x2, x3, w_own, w_other, out, scaled):
    rows = scaled.shape[0]
    squares = jnp.zeros((rows, LANES), f32)
    for chip, block in enumerate((x0, x1, x2, x3)):
        for core in (0, 1):
            vals = block[core, :rows].astype(f32)
            gain = block[core, rows:].astype(f32)[:1]
            squares += vals * vals
            place = (jnp.bitwise_xor(at[1], chip) * 2 + jnp.bitwise_xor(at[0], core)) * LANES
            scaled[:, pl.ds(pl.multiple_of(place, LANES), LANES)] = (vals * gain).astype(bf16)
    total = lax.dot_general(
        jnp.ones((8, LANES), f32),
        squares,
        (((1,), (1,)), ((), ())),
        precision=lax.Precision.HIGHEST,
        preferred_element_type=f32,
    )
    hi = total.astype(bf16).astype(f32)
    mid = (total - hi).astype(bf16).astype(f32)
    row = lax.broadcasted_iota(jnp.int32, (8, rows), 0)
    extra = jnp.where(row == 4, hi, jnp.where(row == 5, mid, jnp.where(row == 6, total - hi - mid, 0.0)))
    extra = jnp.concatenate((jnp.zeros((48, rows), f32), extra, jnp.zeros((56, rows), f32)))
    right = scaled[...]
    for side, weight in enumerate((w_own, w_other)):
        part = lax.dot_general(
            weight[...].reshape(8 * 112, 1024),
            right,
            (((1,), (1,)), ((), ())),
            preferred_element_type=f32,
        ).reshape(8, 112, rows)
        if side == 0:
            part = part + extra[None]
        out[:, side] = part.astype(bf16)


def acts_kernel(at, sums, out):
    rows = sums.shape[-1]
    own = sums[0, 0].astype(f32)
    other = sums[0, 1].astype(f32)
    for part in range(1, 8):
        own += sums[part, 0].astype(f32)
        other += sums[part, 1].astype(f32)
    row = lax.broadcasted_iota(jnp.int32, (8, rows), 0)
    squares = jnp.where((row >= 4) & (row < 7), own[48:56], 0.0)
    inv_rms = lax.rsqrt(jnp.sum(squares, 0, keepdims=True) / FEAT + EPS)
    unit = lax.broadcasted_iota(jnp.int32, (56, rows), 0)
    for side, total in enumerate((own, other)):
        gate = total[:56] * inv_rms
        acts = gate / (1.0 + jnp.exp(-gate)) * (total[56:] * inv_rms)
        acts = jnp.where(unit < 52, acts, 0.0).astype(bf16)
        for copy in range(4):
            out[copy, jnp.bitwise_xor(at[0], side)] = acts


def place_kernel(at, parts, out):
    total = parts[0].astype(f32)
    for part in range(1, 8):
        total += parts[part].astype(f32)
    for piece in range(16):
        column = piece * LANES
        out[jnp.bitwise_xor(at[2], piece)] = total[:, column : column + LANES].astype(bf16)


def run(kernel, out_shape, operands, scratch=(), flops=0):
    moved = sum(o.size * o.dtype.itemsize for o in operands) + int(np.prod(out_shape)) * 2
    return pl.pallas_call(
        kernel,
        out_shape=jax.ShapeDtypeStruct(out_shape, bf16),
        in_specs=[pl.BlockSpec(memory_space=pltpu.SMEM)]
        + [pl.BlockSpec(memory_space=pltpu.VMEM)] * (len(operands) - 1),
        out_specs=pl.BlockSpec(memory_space=pltpu.VMEM),
        scratch_shapes=list(scratch),
        compiler_params=pltpu.CompilerParams(vmem_limit_bytes=40 * 2**20),
        cost_estimate=pl.CostEstimate(flops=flops, bytes_accessed=moved, transcendentals=0),
    )(*operands)


def local(layer_input, norm_gain, gate_weight, up_weight, down_weight):
    phase, core = lax.axis_index(PHASE), lax.axis_index("core")
    at = (core, lax.axis_index(("xl", "z0")), lax.axis_index((*BLOCK, "core")))
    at = jnp.stack(at).astype(jnp.int32)
    units = gate_weight.shape[0]
    rows = layer_input.shape[0] // 2

    halves = layer_input.reshape(8, 2, rows // 8, LANES)
    gain = jnp.broadcast_to(norm_gain[None], (PAD, LANES))

    def half(index):
        part = lax.dynamic_slice_in_dim(halves, index, 1, 1).reshape(rows, LANES)
        return jnp.concatenate((part, gain))

    both = jnp.stack((gate_weight, up_weight))
    both = jnp.pad(both, ((0, 0), (0, 56 - units), (0, 0))).reshape(112, FEAT)
    own_w = exchange(run(cut_kernel, (8, 112, 1024), (at, both)), PHASE)
    first = send(half(core), spread(0, 0))
    second = send(half(1 - core), spread(4, 1))
    first, second, own_w = lax.optimization_barrier((first, second, own_w))
    other_w = send(own_w, shift(core=1))
    held = jnp.stack((first, second))
    blocks = [held] + [send(held, shift(xl=i, z0=j)) for i, j in ((0, 1), (1, 0), (1, 1))]

    down, _ = lax.optimization_barrier((down_weight, held))
    down = jnp.pad(down.reshape(64, units, LANES), ((0, 0), (0, 56 - units), (0, 0)))
    down = down.reshape(2, 4, 2, 2, 112, LANES).transpose(3, 2, 0, 1, 4, 5).reshape(2, 2, 2, 448, LANES)

    def halve(value, axis):
        place = lax.axis_index(axis)
        kept, sent = (
            lax.dynamic_index_in_dim(value, i, 0, keepdims=False) for i in (place, 1 - place)
        )
        return kept, send(sent, shift(**{axis: 1}))

    down = jnp.stack(halve(down, "z0"), 2)
    down = jnp.stack(halve(down, "zm"), 1)

    sums = run(
        sums_kernel,
        (8, 2, 112, rows),
        (at, *blocks, own_w, other_w),
        (pltpu.VMEM((rows, 1024), bf16),),
        flops=2 * 1792 * 1024 * rows,
    )
    sums, down = lax.optimization_barrier((exchange(sums, PHASE), down))
    down = jnp.stack(halve(down, "xl")).reshape(8, 448, LANES)
    down = jnp.stack((down, send(down, shift(core=1))), 1)
    down = down.transpose(2, 0, 1, 3).reshape(448, 2048)
    acts = run(acts_kernel, (4, 2, 56, rows), (at, sums))
    acts = exchange(acts.reshape(4, 112, rows), FAR).reshape(448, rows)
    partials = lax.dot_general(
        acts, down, (((0,), (0,)), ((), ())), preferred_element_type=f32
    ).astype(bf16)
    partials = exchange(partials.reshape(8, rows // 8, 2048), PHASE)
    partials = run(place_kernel, (16, rows // 8, LANES), (at, partials))
    partials = exchange(partials, (*BLOCK, "core")).astype(f32)
    ffn_out = jnp.sum(partials.reshape(8, rows // 4, LANES), 0)
    residual = lax.dynamic_slice_in_dim(layer_input, phase * (rows // 4), rows // 4, 0)
    return (residual.astype(f32) + ffn_out).astype(bf16)


def solution(mesh):
    fine = Mesh(mesh.devices.reshape(SIZES), AXES)
    return jax.shard_map(
        local,
        mesh=fine,
        in_specs=(
            P(None, BLK),
            P(BLK),
            P((*PHASE, *BLK), None),
            P((*PHASE, *BLK), None),
            P(PHASE, BLK),
        ),
        out_specs=P(PHASE, BLK),
        check_vma=False,
    )
```

```python
import jax
import jax.numpy as jnp
import numpy as np
from jax import lax
from jax.experimental import pallas as pl
from jax.experimental.pallas import tpu as pltpu
from jax.sharding import Mesh, PartitionSpec as P

FEAT = 8192
EPS = 1e-05
LANES = 128
PAD = 16

AXES = ("y", "xh", "xl", "zh", "zm", "z0", "core")
SIZES = (4, 2, 2, 4, 2, 2, 2)
PHASE = ("y", "xh")
BLK = ("xl", "zh", "zm", "z0", "core")
FAR = "zh"
BLOCK = ("xl", "zm", "z0")

f32, bf16 = jnp.float32, jnp.bfloat16


def exchange(value, axes):
    return lax.all_to_all(value, axes, 0, 0, tiled=True)


def route(move):
    pairs = []
    for at in np.ndindex(*SIZES):
        to = dict(zip(AXES, at))
        move(to)
        to = tuple(to[a] % n for a, n in zip(AXES, SIZES))
        pairs.append([int(np.ravel_multi_index(i, SIZES)) for i in (at, to)])
    return pairs


def send(value, move):
    return lax.ppermute(value, AXES, route(move))


def spread(turn, cross):
    def move(to):
        part, group = to["y"] * 2 + to["xh"], to["zh"] * 2 + to["zm"]
        to["y"], to["xh"] = divmod(group, 2)
        to["zh"], to["zm"] = divmod((part + turn - group) % 8, 2)
        to["core"] += cross

    return move


def shift(**by):
    def move(to):
        for axis, count in by.items():
            to[axis] += count

    return move


def cut_kernel(at, both, out):
    del at
    for group in range(8):
        for side in (0, 1):
            start = side * FEAT // 2 + group * 512
            out[group, :, side * 512 : side * 512 + 512] = both[:, start : start + 512]


def sums_kernel(at, x0, x1, x2, x3, w_own, w_other, out, scaled):
    rows = scaled.shape[0]
    squares = jnp.zeros((rows, LANES), f32)
    for chip, block in enumerate((x0, x1, x2, x3)):
        for core in (0, 1):
            vals = block[core, :rows].astype(f32)
            gain = block[core, rows:].astype(f32)[:1]
            squares += vals * vals
            place = (jnp.bitwise_xor(at[1], chip) * 2 + jnp.bitwise_xor(at[0], core)) * LANES
            scaled[:, pl.ds(pl.multiple_of(place, LANES), LANES)] = (vals * gain).astype(bf16)
    total = lax.dot_general(
        jnp.ones((8, LANES), f32),
        squares,
        (((1,), (1,)), ((), ())),
        precision=lax.Precision.HIGHEST,
        preferred_element_type=f32,
    )
    hi = total.astype(bf16).astype(f32)
    mid = (total - hi).astype(bf16).astype(f32)
    row = lax.broadcasted_iota(jnp.int32, (8, rows), 0)
    extra = jnp.where(row == 4, hi, jnp.where(row == 5, mid, jnp.where(row == 6, total - hi - mid, 0.0)))
    extra = jnp.concatenate((jnp.zeros((48, rows), f32), extra, jnp.zeros((56, rows), f32)))
    right = scaled[...]
    for side, weight in enumerate((w_own, w_other)):
        part = lax.dot_general(
            weight[...].reshape(8 * 112, 1024),
            right,
            (((1,), (1,)), ((), ())),
            preferred_element_type=f32,
        ).reshape(8, 112, rows)
        if side == 0:
            part = part + extra[None]
        out[:, side] = part.astype(bf16)


def acts_kernel(at, sums, out):
    rows = sums.shape[-1]
    own = sums[0, 0].astype(f32)
    other = sums[0, 1].astype(f32)
    for part in range(1, 8):
        own += sums[part, 0].astype(f32)
        other += sums[part, 1].astype(f32)
    row = lax.broadcasted_iota(jnp.int32, (8, rows), 0)
    squares = jnp.where((row >= 4) & (row < 7), own[48:56], 0.0)
    inv_rms = lax.rsqrt(jnp.sum(squares, 0, keepdims=True) / FEAT + EPS)
    unit = lax.broadcasted_iota(jnp.int32, (56, rows), 0)
    for side, total in enumerate((own, other)):
        gate = total[:56] * inv_rms
        acts = gate / (1.0 + jnp.exp(-gate)) * (total[56:] * inv_rms)
        acts = jnp.where(unit < 52, acts, 0.0).astype(bf16)
        for copy in range(4):
            out[copy, jnp.bitwise_xor(at[0], side)] = acts


def place_kernel(at, parts, out):
    total = parts[0].astype(f32)
    for part in range(1, 8):
        total += parts[part].astype(f32)
    for piece in range(16):
        column = piece * LANES
        out[jnp.bitwise_xor(at[2], piece)] = total[:, column : column + LANES].astype(bf16)


def run(kernel, out_shape, operands, scratch=(), flops=0):
    moved = sum(o.size * o.dtype.itemsize for o in operands) + int(np.prod(out_shape)) * 2
    return pl.pallas_call(
        kernel,
        out_shape=jax.ShapeDtypeStruct(out_shape, bf16),
        in_specs=[pl.BlockSpec(memory_space=pltpu.SMEM)]
        + [pl.BlockSpec(memory_space=pltpu.VMEM)] * (len(operands) - 1),
        out_specs=pl.BlockSpec(memory_space=pltpu.VMEM),
        scratch_shapes=list(scratch),
        compiler_params=pltpu.CompilerParams(vmem_limit_bytes=40 * 2**20),
        cost_estimate=pl.CostEstimate(flops=flops, bytes_accessed=moved, transcendentals=0),
    )(*operands)


def local(layer_input, norm_gain, gate_weight, up_weight, down_weight):
    phase, core = lax.axis_index(PHASE), lax.axis_index("core")
    at = (core, lax.axis_index(("xl", "z0")), lax.axis_index((*BLOCK, "core")))
    at = jnp.stack(at).astype(jnp.int32)
    units = gate_weight.shape[0]
    rows = layer_input.shape[0] // 2

    halves = layer_input.reshape(8, 2, rows // 8, LANES)
    gain = jnp.broadcast_to(norm_gain[None], (PAD, LANES))

    def half(index):
        part = lax.dynamic_slice_in_dim(halves, index, 1, 1).reshape(rows, LANES)
        return jnp.concatenate((part, gain))

    down = jnp.pad(down_weight.reshape(64, units, LANES), ((0, 0), (0, 56 - units), (0, 0)))
    down = down.reshape(2, 4, 2, 2, 112, LANES).transpose(3, 2, 0, 1, 4, 5).reshape(2, 2, 2, 448, LANES)

    both = jnp.stack((gate_weight, up_weight))
    both = jnp.pad(both, ((0, 0), (0, 56 - units), (0, 0))).reshape(112, FEAT)
    own_w = exchange(run(cut_kernel, (8, 112, 1024), (at, both)), PHASE)
    first = send(half(core), spread(0, 0))
    second = send(half(1 - core), spread(4, 1))
    first, second, own_w, down = lax.optimization_barrier((first, second, own_w, down))
    other_w = send(own_w, shift(core=1))
    held = jnp.stack((first, second))
    blocks = [held] + [send(held, shift(xl=i, z0=j)) for i, j in ((0, 1), (1, 0), (1, 1))]

    def halve(value, axis):
        place = lax.axis_index(axis)
        kept, sent = (
            lax.dynamic_index_in_dim(value, i, 0, keepdims=False) for i in (place, 1 - place)
        )
        return kept, send(sent, shift(**{axis: 1}))

    down = jnp.stack(halve(down, "z0"), 2)
    sums = run(
        sums_kernel,
        (8, 2, 112, rows),
        (at, *blocks, own_w, other_w),
        (pltpu.VMEM((rows, 1024), bf16),),
        flops=2 * 1792 * 1024 * rows,
    )
    sums, down = lax.optimization_barrier((sums, down))
    down = jnp.stack(halve(down, "zm"), 1)
    sums, down = lax.optimization_barrier((exchange(sums, PHASE), down))
    down = jnp.stack(halve(down, "xl")).reshape(8, 448, LANES)
    down = jnp.stack((down, send(down, shift(core=1))), 1)
    down = down.transpose(2, 0, 1, 3).reshape(448, 2048)
    acts = run(acts_kernel, (4, 2, 56, rows), (at, sums))
    acts = exchange(acts.reshape(4, 112, rows), FAR).reshape(448, rows)
    partials = lax.dot_general(
        acts, down, (((0,), (0,)), ((), ())), preferred_element_type=f32
    ).astype(bf16)
    partials = exchange(partials.reshape(8, rows // 8, 2048), PHASE)
    partials = run(place_kernel, (16, rows // 8, LANES), (at, partials))
    partials = exchange(partials, (*BLOCK, "core")).astype(f32)
    ffn_out = jnp.sum(partials.reshape(8, rows // 4, LANES), 0)
    residual = lax.dynamic_slice_in_dim(layer_input, phase * (rows // 4), rows // 4, 0)
    return (residual.astype(f32) + ffn_out).astype(bf16)


def solution(mesh):
    fine = Mesh(mesh.devices.reshape(SIZES), AXES)
    return jax.shard_map(
        local,
        mesh=fine,
        in_specs=(
            P(None, BLK),
            P(BLK),
            P((*PHASE, *BLK), None),
            P((*PHASE, *BLK), None),
            P(PHASE, BLK),
        ),
        out_specs=P(PHASE, BLK),
        check_vma=False,
    )
```

```python
import jax
import jax.numpy as jnp
import numpy as np
from jax import lax
from jax.experimental import pallas as pl
from jax.experimental.pallas import tpu as pltpu
from jax.sharding import Mesh, PartitionSpec as P

FEAT = 8192
EPS = 1e-05
LANES = 128
PAD = 16

AXES = ("y", "xh", "xl", "zh", "zm", "z0", "core")
SIZES = (4, 2, 2, 4, 2, 2, 2)
PHASE = ("y", "xh")
BLK = ("xl", "zh", "zm", "z0", "core")
FAR = "zh"
BLOCK = ("xl", "zm", "z0")

f32, bf16 = jnp.float32, jnp.bfloat16


def exchange(value, axes):
    return lax.all_to_all(value, axes, 0, 0, tiled=True)


def route(move):
    pairs = []
    for at in np.ndindex(*SIZES):
        to = dict(zip(AXES, at))
        move(to)
        to = tuple(to[a] % n for a, n in zip(AXES, SIZES))
        pairs.append([int(np.ravel_multi_index(i, SIZES)) for i in (at, to)])
    return pairs


def send(value, move):
    return lax.ppermute(value, AXES, route(move))


def spread(turn, cross):
    def move(to):
        part, group = to["y"] * 2 + to["xh"], to["zh"] * 2 + to["zm"]
        to["y"], to["xh"] = divmod(group, 2)
        to["zh"], to["zm"] = divmod((part + turn - group) % 8, 2)
        to["core"] += cross

    return move


def shift(**by):
    def move(to):
        for axis, count in by.items():
            to[axis] += count

    return move


def cut_kernel(at, both, out):
    del at
    for group in range(8):
        for side in (0, 1):
            start = side * FEAT // 2 + group * 512
            out[group, :, side * 512 : side * 512 + 512] = both[:, start : start + 512]


def sums_kernel(at, x0, x1, x2, x3, w_own, w_other, out, scaled):
    rows = scaled.shape[0]
    squares = jnp.zeros((rows, LANES), f32)
    for chip, block in enumerate((x0, x1, x2, x3)):
        for core in (0, 1):
            vals = block[core, :rows].astype(f32)
            gain = block[core, rows:].astype(f32)[:1]
            squares += vals * vals
            place = (jnp.bitwise_xor(at[1], chip) * 2 + jnp.bitwise_xor(at[0], core)) * LANES
            scaled[:, pl.ds(pl.multiple_of(place, LANES), LANES)] = (vals * gain).astype(bf16)
    total = lax.dot_general(
        jnp.ones((8, LANES), f32),
        squares,
        (((1,), (1,)), ((), ())),
        precision=lax.Precision.HIGHEST,
        preferred_element_type=f32,
    )
    hi = total.astype(bf16).astype(f32)
    mid = (total - hi).astype(bf16).astype(f32)
    row = lax.broadcasted_iota(jnp.int32, (8, rows), 0)
    extra = jnp.where(row == 4, hi, jnp.where(row == 5, mid, jnp.where(row == 6, total - hi - mid, 0.0)))
    extra = jnp.concatenate((jnp.zeros((48, rows), f32), extra, jnp.zeros((56, rows), f32)))
    right = scaled[...]
    for side, weight in enumerate((w_own, w_other)):
        part = lax.dot_general(
            weight[...].reshape(8 * 112, 1024),
            right,
            (((1,), (1,)), ((), ())),
            preferred_element_type=f32,
        ).reshape(8, 112, rows)
        if side == 0:
            part = part + extra[None]
        out[:, side] = part.astype(bf16)


def acts_kernel(at, sums, out):
    rows = sums.shape[-1]
    own = sums[0, 0].astype(f32)
    other = sums[0, 1].astype(f32)
    for part in range(1, 8):
        own += sums[part, 0].astype(f32)
        other += sums[part, 1].astype(f32)
    row = lax.broadcasted_iota(jnp.int32, (8, rows), 0)
    squares = jnp.where((row >= 4) & (row < 7), own[48:56], 0.0)
    inv_rms = lax.rsqrt(jnp.sum(squares, 0, keepdims=True) / FEAT + EPS)
    unit = lax.broadcasted_iota(jnp.int32, (56, rows), 0)
    for side, total in enumerate((own, other)):
        gate = total[:56] * inv_rms
        acts = gate / (1.0 + jnp.exp(-gate)) * (total[56:] * inv_rms)
        acts = jnp.where(unit < 52, acts, 0.0).astype(bf16)
        for copy in range(4):
            out[copy, jnp.bitwise_xor(at[0], side)] = acts


def place_kernel(at, parts, out):
    total = parts[0].astype(f32)
    for part in range(1, 8):
        total += parts[part].astype(f32)
    for piece in range(16):
        column = piece * LANES
        out[jnp.bitwise_xor(at[2], piece)] = total[:, column : column + LANES].astype(bf16)


def run(kernel, out_shape, operands, scratch=(), flops=0):
    moved = sum(o.size * o.dtype.itemsize for o in operands) + int(np.prod(out_shape)) * 2
    return pl.pallas_call(
        kernel,
        out_shape=jax.ShapeDtypeStruct(out_shape, bf16),
        in_specs=[pl.BlockSpec(memory_space=pltpu.SMEM)]
        + [pl.BlockSpec(memory_space=pltpu.VMEM)] * (len(operands) - 1),
        out_specs=pl.BlockSpec(memory_space=pltpu.VMEM),
        scratch_shapes=list(scratch),
        compiler_params=pltpu.CompilerParams(vmem_limit_bytes=40 * 2**20),
        cost_estimate=pl.CostEstimate(flops=flops, bytes_accessed=moved, transcendentals=0),
    )(*operands)


def local(layer_input, norm_gain, gate_weight, up_weight, down_weight):
    phase, core = lax.axis_index(PHASE), lax.axis_index("core")
    at = (core, lax.axis_index(("xl", "z0")), lax.axis_index((*BLOCK, "core")))
    at = jnp.stack(at).astype(jnp.int32)
    units = gate_weight.shape[0]
    rows = layer_input.shape[0] // 2

    halves = layer_input.reshape(8, 2, rows // 8, LANES)
    gain = jnp.broadcast_to(norm_gain[None], (PAD, LANES))

    def half(index):
        part = lax.dynamic_slice_in_dim(halves, index, 1, 1).reshape(rows, LANES)
        return jnp.concatenate((part, gain))

    def halve(value, axis):
        place = lax.axis_index(axis)
        kept, sent = (
            lax.dynamic_index_in_dim(value, i, 0, keepdims=False) for i in (place, 1 - place)
        )
        return kept, send(sent, shift(**{axis: 1}))

    down = jnp.pad(down_weight.reshape(64, units, LANES), ((0, 0), (0, 56 - units), (0, 0)))
    down = down.reshape(2, 4, 2, 2, 112, LANES).transpose(3, 2, 0, 1, 4, 5).reshape(2, 2, 2, 448, LANES)
    down = jnp.stack(halve(down, "z0"), 2)

    both = jnp.stack((gate_weight, up_weight))
    both = jnp.pad(both, ((0, 0), (0, 56 - units), (0, 0))).reshape(112, FEAT)
    own_w = exchange(run(cut_kernel, (8, 112, 1024), (at, both)), PHASE)
    first = send(half(core), spread(0, 0))
    second = send(half(1 - core), spread(4, 1))
    first, second, own_w, down = lax.optimization_barrier((first, second, own_w, down))
    other_w = send(own_w, shift(core=1))
    held = jnp.stack((first, second))
    blocks = [held] + [send(held, shift(xl=i, z0=j)) for i, j in ((0, 1), (1, 0), (1, 1))]

    sums = run(
        sums_kernel,
        (8, 2, 112, rows),
        (at, *blocks, own_w, other_w),
        (pltpu.VMEM((rows, 1024), bf16),),
        flops=2 * 1792 * 1024 * rows,
    )
    sums, down = lax.optimization_barrier((sums, down))
    down = jnp.stack(halve(down, "zm"), 1)
    sums, down = lax.optimization_barrier((exchange(sums, PHASE), down))
    down = jnp.stack(halve(down, "xl")).reshape(8, 448, LANES)
    down = jnp.stack((down, send(down, shift(core=1))), 1)
    down = down.transpose(2, 0, 1, 3).reshape(448, 2048)
    acts = run(acts_kernel, (4, 2, 56, rows), (at, sums))
    acts = exchange(acts.reshape(4, 112, rows), FAR).reshape(448, rows)
    partials = lax.dot_general(
        acts, down, (((0,), (0,)), ((), ())), preferred_element_type=f32
    ).astype(bf16)
    partials = exchange(partials.reshape(8, rows // 8, 2048), PHASE)
    partials = run(place_kernel, (16, rows // 8, LANES), (at, partials))
    partials = exchange(partials, (*BLOCK, "core")).astype(f32)
    ffn_out = jnp.sum(partials.reshape(8, rows // 4, LANES), 0)
    residual = lax.dynamic_slice_in_dim(layer_input, phase * (rows // 4), rows // 4, 0)
    return (residual.astype(f32) + ffn_out).astype(bf16)


def solution(mesh):
    fine = Mesh(mesh.devices.reshape(SIZES), AXES)
    return jax.shard_map(
        local,
        mesh=fine,
        in_specs=(
            P(None, BLK),
            P(BLK),
            P((*PHASE, *BLK), None),
            P((*PHASE, *BLK), None),
            P(PHASE, BLK),
        ),
        out_specs=P(PHASE, BLK),
        check_vma=False,
    )
```

```python
import jax
import jax.numpy as jnp
import numpy as np
from jax import lax
from jax.experimental import pallas as pl
from jax.experimental.pallas import tpu as pltpu
from jax.sharding import Mesh, PartitionSpec as P

FEAT = 8192
EPS = 1e-05
LANES = 128
PAD = 16

AXES = ("y", "xh", "xl", "zh", "zm", "z0", "core")
SIZES = (4, 2, 2, 4, 2, 2, 2)
PHASE = ("y", "xh")
BLK = ("xl", "zh", "zm", "z0", "core")
FAR = "zh"
BLOCK = ("xl", "zm", "z0")

f32, bf16 = jnp.float32, jnp.bfloat16


def exchange(value, axes):
    return lax.all_to_all(value, axes, 0, 0, tiled=True)


def route(move):
    pairs = []
    for at in np.ndindex(*SIZES):
        to = dict(zip(AXES, at))
        move(to)
        to = tuple(to[a] % n for a, n in zip(AXES, SIZES))
        pairs.append([int(np.ravel_multi_index(i, SIZES)) for i in (at, to)])
    return pairs


def send(value, move):
    return lax.ppermute(value, AXES, route(move))


def spread(turn, cross):
    def move(to):
        part, group = to["y"] * 2 + to["xh"], to["zh"] * 2 + to["zm"]
        to["y"], to["xh"] = divmod(group, 2)
        to["zh"], to["zm"] = divmod((part + turn - group) % 8, 2)
        to["core"] += cross

    return move


def shift(**by):
    def move(to):
        for axis, count in by.items():
            to[axis] += count

    return move


def cut_kernel(at, gate, up, out):
    del at
    zero = jnp.zeros((56 - gate.shape[0], 512), f32)
    for group in range(8):
        for side in (0, 1):
            start = side * FEAT // 2 + group * 512
            parts = (gate[:, start : start + 512].astype(f32), zero, up[:, start : start + 512].astype(f32), zero)
            out[group, :, side * 512 : side * 512 + 512] = jnp.concatenate(parts).astype(bf16)


def sums_kernel(at, x0, x1, x2, x3, w_own, w_other, out, scaled):
    rows = scaled.shape[0]
    squares = jnp.zeros((rows, LANES), f32)
    for chip, block in enumerate((x0, x1, x2, x3)):
        for core in (0, 1):
            vals = block[core, :rows].astype(f32)
            gain = block[core, rows:].astype(f32)[:1]
            squares += vals * vals
            place = (jnp.bitwise_xor(at[1], chip) * 2 + jnp.bitwise_xor(at[0], core)) * LANES
            scaled[:, pl.ds(pl.multiple_of(place, LANES), LANES)] = (vals * gain).astype(bf16)
    total = lax.dot_general(
        jnp.ones((8, LANES), f32),
        squares,
        (((1,), (1,)), ((), ())),
        precision=lax.Precision.HIGHEST,
        preferred_element_type=f32,
    )
    hi = total.astype(bf16).astype(f32)
    mid = (total - hi).astype(bf16).astype(f32)
    row = lax.broadcasted_iota(jnp.int32, (8, rows), 0)
    extra = jnp.where(row == 4, hi, jnp.where(row == 5, mid, jnp.where(row == 6, total - hi - mid, 0.0)))
    extra = jnp.concatenate((jnp.zeros((48, rows), f32), extra, jnp.zeros((56, rows), f32)))
    right = scaled[...]
    for side, weight in enumerate((w_own, w_other)):
        part = lax.dot_general(
            weight[...].reshape(8 * 112, 1024),
            right,
            (((1,), (1,)), ((), ())),
            preferred_element_type=f32,
        ).reshape(8, 112, rows)
        if side == 0:
            part = part + extra[None]
        out[:, side] = part.astype(bf16)


def acts_kernel(at, sums, out):
    rows = sums.shape[-1]
    own = sums[0, 0].astype(f32)
    other = sums[0, 1].astype(f32)
    for part in range(1, 8):
        own += sums[part, 0].astype(f32)
        other += sums[part, 1].astype(f32)
    row = lax.broadcasted_iota(jnp.int32, (8, rows), 0)
    squares = jnp.where((row >= 4) & (row < 7), own[48:56], 0.0)
    inv_rms = lax.rsqrt(jnp.sum(squares, 0, keepdims=True) / FEAT + EPS)
    unit = lax.broadcasted_iota(jnp.int32, (56, rows), 0)
    for side, total in enumerate((own, other)):
        gate = total[:56] * inv_rms
        acts = gate / (1.0 + jnp.exp(-gate)) * (total[56:] * inv_rms)
        acts = jnp.where(unit < 52, acts, 0.0).astype(bf16)
        for copy in range(4):
            out[copy, jnp.bitwise_xor(at[0], side)] = acts


def place_kernel(at, parts, out):
    total = parts[0].astype(f32)
    for part in range(1, 8):
        total += parts[part].astype(f32)
    for piece in range(16):
        column = piece * LANES
        out[jnp.bitwise_xor(at[2], piece)] = total[:, column : column + LANES].astype(bf16)


def run(kernel, out_shape, operands, scratch=(), flops=0):
    moved = sum(o.size * o.dtype.itemsize for o in operands) + int(np.prod(out_shape)) * 2
    return pl.pallas_call(
        kernel,
        out_shape=jax.ShapeDtypeStruct(out_shape, bf16),
        in_specs=[pl.BlockSpec(memory_space=pltpu.SMEM)]
        + [pl.BlockSpec(memory_space=pltpu.VMEM)] * (len(operands) - 1),
        out_specs=pl.BlockSpec(memory_space=pltpu.VMEM),
        scratch_shapes=list(scratch),
        compiler_params=pltpu.CompilerParams(vmem_limit_bytes=40 * 2**20),
        cost_estimate=pl.CostEstimate(flops=flops, bytes_accessed=moved, transcendentals=0),
    )(*operands)


def local(layer_input, norm_gain, gate_weight, up_weight, down_weight):
    phase, core = lax.axis_index(PHASE), lax.axis_index("core")
    at = (core, lax.axis_index(("xl", "z0")), lax.axis_index((*BLOCK, "core")))
    at = jnp.stack(at).astype(jnp.int32)
    units = gate_weight.shape[0]
    rows = layer_input.shape[0] // 2

    halves = layer_input.reshape(8, 2, rows // 8, LANES)
    gain = jnp.broadcast_to(norm_gain[None], (PAD, LANES))

    def half(index):
        part = lax.dynamic_slice_in_dim(halves, index, 1, 1).reshape(rows, LANES)
        return jnp.concatenate((part, gain))

    def halve(value, axis):
        place = lax.axis_index(axis)
        kept, sent = (
            lax.dynamic_index_in_dim(value, i, 0, keepdims=False) for i in (place, 1 - place)
        )
        return kept, send(sent, shift(**{axis: 1}))

    down = jnp.pad(down_weight.reshape(64, units, LANES), ((0, 0), (0, 56 - units), (0, 0)))
    down = down.reshape(2, 4, 2, 2, 112, LANES).transpose(3, 2, 0, 1, 4, 5).reshape(2, 2, 2, 448, LANES)
    down = jnp.stack(halve(down, "z0"), 2)

    own_w = exchange(run(cut_kernel, (8, 112, 1024), (at, gate_weight, up_weight)), PHASE)
    first = send(half(core), spread(0, 0))
    second = send(half(1 - core), spread(4, 1))
    first, second, own_w, down = lax.optimization_barrier((first, second, own_w, down))
    other_w = send(own_w, shift(core=1))
    held = jnp.stack((first, second))
    blocks = [held] + [send(held, shift(xl=i, z0=j)) for i, j in ((0, 1), (1, 0), (1, 1))]

    sums = run(
        sums_kernel,
        (8, 2, 112, rows),
        (at, *blocks, own_w, other_w),
        (pltpu.VMEM((rows, 1024), bf16),),
        flops=2 * 1792 * 1024 * rows,
    )
    kept, got = halve(down, "zm")
    acts = run(acts_kernel, (4, 2, 56, rows), (at, exchange(sums, PHASE)))
    acts, got = lax.optimization_barrier((acts, got))
    (kept0, got0), (kept1, got1) = halve(kept, "xl"), halve(got, "xl")
    down = jnp.stack((kept0, kept1, got0, got1)).reshape(8, 448, LANES)
    down = jnp.stack((down, send(down, shift(core=1))), 1)
    down = down.transpose(2, 0, 1, 3).reshape(448, 2048)
    acts = exchange(acts.reshape(4, 112, rows), FAR).reshape(448, rows)
    partials = lax.dot_general(
        acts, down, (((0,), (0,)), ((), ())), preferred_element_type=f32
    ).astype(bf16)
    partials = exchange(partials.reshape(8, rows // 8, 2048), PHASE)
    partials = run(place_kernel, (16, rows // 8, LANES), (at, partials))
    partials = exchange(partials, (*BLOCK, "core")).astype(f32)
    ffn_out = jnp.sum(partials.reshape(8, rows // 4, LANES), 0)
    residual = lax.dynamic_slice_in_dim(layer_input, phase * (rows // 4), rows // 4, 0)
    return (residual.astype(f32) + ffn_out).astype(bf16)


def solution(mesh):
    fine = Mesh(mesh.devices.reshape(SIZES), AXES)
    return jax.shard_map(
        local,
        mesh=fine,
        in_specs=(
            P(None, BLK),
            P(BLK),
            P((*PHASE, *BLK), None),
            P((*PHASE, *BLK), None),
            P(PHASE, BLK),
        ),
        out_specs=P(PHASE, BLK),
        check_vma=False,
    )
```

```python
import jax
import jax.numpy as jnp
import numpy as np
from jax import lax
from jax.experimental import pallas as pl
from jax.experimental.pallas import tpu as pltpu
from jax.sharding import Mesh, PartitionSpec as P

FEAT = 8192
EPS = 1e-05
LANES = 128
PAD = 16

AXES = ("y", "xh", "xl", "zh", "zm", "z0", "core")
SIZES = (4, 2, 2, 4, 2, 2, 2)
PHASE = ("y", "xh")
BLK = ("xl", "zh", "zm", "z0", "core")
FAR = "zh"
BLOCK = ("xl", "zm", "z0")

f32, bf16 = jnp.float32, jnp.bfloat16


def exchange(value, axes):
    return lax.all_to_all(value, axes, 0, 0, tiled=True)


def route(move):
    pairs = []
    for at in np.ndindex(*SIZES):
        to = dict(zip(AXES, at))
        move(to)
        to = tuple(to[a] % n for a, n in zip(AXES, SIZES))
        pairs.append([int(np.ravel_multi_index(i, SIZES)) for i in (at, to)])
    return pairs


def send(value, move):
    return lax.ppermute(value, AXES, route(move))


def spread(turn, cross):
    def move(to):
        part, group = to["y"] * 2 + to["xh"], to["zh"] * 2 + to["zm"]
        to["y"], to["xh"] = divmod(group, 2)
        to["zh"], to["zm"] = divmod((part + turn - group) % 8, 2)
        to["core"] += cross

    return move


def shift(**by):
    def move(to):
        for axis, count in by.items():
            to[axis] += count

    return move


def cut_kernel(gate, up, out):
    zero = jnp.zeros((56 - gate.shape[0], 512), f32)
    for group in range(4):
        columns = slice(group * 512, group * 512 + 512)
        parts = (gate[:, columns].astype(f32), zero, up[:, columns].astype(f32), zero)
        out[group] = jnp.concatenate(parts).astype(bf16)


def cut(gate, up):
    units = gate.shape[0]
    return pl.pallas_call(
        cut_kernel,
        grid=(4,),
        out_shape=jax.ShapeDtypeStruct((8, 112, 1024), bf16),
        in_specs=[pl.BlockSpec((units, 2048), lambda i: (0, i))] * 2,
        out_specs=pl.BlockSpec((4, 112, 512), lambda i: (i % 2, 0, i // 2)),
        compiler_params=pltpu.CompilerParams(vmem_limit_bytes=60 * 2**20),
        cost_estimate=pl.CostEstimate(flops=0, bytes_accessed=8 * units * FEAT, transcendentals=0),
    )(gate, up)


def sums_kernel(at, x0, x1, x2, x3, w_own, w_other, out, scaled):
    rows = scaled.shape[0]
    squares = jnp.zeros((rows, LANES), f32)
    for chip, block in enumerate((x0, x1, x2, x3)):
        for core in (0, 1):
            vals = block[core, :rows].astype(f32)
            gain = block[core, rows:].astype(f32)[:1]
            squares += vals * vals
            place = (jnp.bitwise_xor(at[1], chip) * 2 + jnp.bitwise_xor(at[0], core)) * LANES
            scaled[:, pl.ds(pl.multiple_of(place, LANES), LANES)] = (vals * gain).astype(bf16)
    total = lax.dot_general(
        jnp.ones((8, LANES), f32),
        squares,
        (((1,), (1,)), ((), ())),
        precision=lax.Precision.HIGHEST,
        preferred_element_type=f32,
    )
    hi = total.astype(bf16).astype(f32)
    mid = (total - hi).astype(bf16).astype(f32)
    row = lax.broadcasted_iota(jnp.int32, (8, rows), 0)
    extra = jnp.where(row == 4, hi, jnp.where(row == 5, mid, jnp.where(row == 6, total - hi - mid, 0.0)))
    extra = jnp.concatenate((jnp.zeros((48, rows), f32), extra, jnp.zeros((56, rows), f32)))
    right = scaled[...]
    for side, weight in enumerate((w_own, w_other)):
        part = lax.dot_general(
            weight[...].reshape(8 * 112, 1024),
            right,
            (((1,), (1,)), ((), ())),
            preferred_element_type=f32,
        ).reshape(8, 112, rows)
        if side == 0:
            part = part + extra[None]
        out[:, side] = part.astype(bf16)


def acts_kernel(at, sums, out):
    rows = sums.shape[-1]
    own = sums[0, 0].astype(f32)
    other = sums[0, 1].astype(f32)
    for part in range(1, 8):
        own += sums[part, 0].astype(f32)
        other += sums[part, 1].astype(f32)
    row = lax.broadcasted_iota(jnp.int32, (8, rows), 0)
    squares = jnp.where((row >= 4) & (row < 7), own[48:56], 0.0)
    inv_rms = lax.rsqrt(jnp.sum(squares, 0, keepdims=True) / FEAT + EPS)
    acts = []
    for total in (own, other):
        gate = total[:52] * inv_rms
        acts.append(gate / (1.0 + jnp.exp(-gate)) * (total[56:108] * inv_rms))
    swapped = at[0] == 1
    acts = (jnp.where(swapped, acts[1], acts[0]), jnp.where(swapped, acts[0], acts[1]))
    acts = jnp.concatenate(acts).astype(bf16)
    for copy in range(4):
        out[copy] = acts


def place_kernel(at, parts, out):
    total = parts[0].astype(f32)
    for part in range(1, 8):
        total += parts[part].astype(f32)
    for piece in range(16):
        column = piece * LANES
        out[jnp.bitwise_xor(at[2], piece)] = total[:, column : column + LANES].astype(bf16)


def run(kernel, out_shape, operands, scratch=(), flops=0, vmem=32):
    moved = sum(o.size * o.dtype.itemsize for o in operands) + int(np.prod(out_shape)) * 2
    return pl.pallas_call(
        kernel,
        out_shape=jax.ShapeDtypeStruct(out_shape, bf16),
        in_specs=[pl.BlockSpec(memory_space=pltpu.SMEM)]
        + [pl.BlockSpec(memory_space=pltpu.VMEM)] * (len(operands) - 1),
        out_specs=pl.BlockSpec(memory_space=pltpu.VMEM),
        scratch_shapes=list(scratch),
        compiler_params=pltpu.CompilerParams(vmem_limit_bytes=vmem * 2**20),
        cost_estimate=pl.CostEstimate(flops=flops, bytes_accessed=moved, transcendentals=0),
    )(*operands)


def local(layer_input, norm_gain, gate_weight, up_weight, down_weight):
    phase, core = lax.axis_index(PHASE), lax.axis_index("core")
    at = (core, lax.axis_index(("xl", "z0")), lax.axis_index((*BLOCK, "core")))
    at = jnp.stack(at).astype(jnp.int32)
    units = gate_weight.shape[0]
    rows = layer_input.shape[0] // 2

    halves = layer_input.reshape(8, 2, rows // 8, LANES)
    gain = jnp.broadcast_to(norm_gain[None], (PAD, LANES))

    def half(index):
        part = lax.dynamic_slice_in_dim(halves, index, 1, 1).reshape(rows, LANES)
        return jnp.concatenate((part, gain))

    def halve(value, axis):
        place = lax.axis_index(axis)
        kept, sent = (
            lax.dynamic_index_in_dim(value, i, 0, keepdims=False) for i in (place, 1 - place)
        )
        return kept, send(sent, shift(**{axis: 1}))

    down = down_weight.reshape(2, 4, 2, 2, 2 * units, LANES)
    down = down.transpose(3, 2, 0, 1, 4, 5).reshape(2, 2, 2, 8 * units, LANES)
    down = jnp.stack(halve(down, "z0"), 2)

    own_w = exchange(cut(gate_weight, up_weight), PHASE)
    first = send(half(core), spread(0, 0))
    second = send(half(1 - core), spread(4, 1))
    first, second, own_w, down = lax.optimization_barrier((first, second, own_w, down))
    other_w = send(own_w, shift(core=1))
    held = jnp.stack((first, second))
    blocks = [held] + [send(held, shift(xl=i, z0=j)) for i, j in ((0, 1), (1, 0), (1, 1))]

    sums = run(
        sums_kernel,
        (8, 2, 112, rows),
        (at, *blocks, own_w, other_w),
        (pltpu.VMEM((rows, 1024), bf16),),
        flops=2 * 1792 * 1024 * rows,
        vmem=60,
    )
    kept, got = halve(down, "zm")
    acts = run(acts_kernel, (4, 2 * units, rows), (at, exchange(sums, PHASE)))
    acts, got = lax.optimization_barrier((acts, got))
    (kept0, got0), (kept1, got1) = halve(kept, "xl"), halve(got, "xl")
    down = jnp.stack((kept0, kept1, got0, got1)).reshape(8, 8 * units, LANES)
    down = jnp.stack((down, send(down, shift(core=1))), 1)
    down = down.transpose(2, 0, 1, 3).reshape(8 * units, 2048)
    acts = exchange(acts, FAR).reshape(8 * units, rows)
    partials = lax.dot_general(
        acts, down, (((0,), (0,)), ((), ())), preferred_element_type=f32
    ).astype(bf16)
    partials = exchange(partials.reshape(8, rows // 8, 2048), PHASE)
    partials = run(place_kernel, (16, rows // 8, LANES), (at, partials))
    partials = exchange(partials, (*BLOCK, "core")).astype(f32)
    ffn_out = jnp.sum(partials.reshape(8, rows // 4, LANES), 0)
    residual = lax.dynamic_slice_in_dim(layer_input, phase * (rows // 4), rows // 4, 0)
    return (residual.astype(f32) + ffn_out).astype(bf16)


def solution(mesh):
    fine = Mesh(mesh.devices.reshape(SIZES), AXES)
    return jax.shard_map(
        local,
        mesh=fine,
        in_specs=(
            P(None, BLK),
            P(BLK),
            P((*PHASE, *BLK), None),
            P((*PHASE, *BLK), None),
            P(PHASE, BLK),
        ),
        out_specs=P(PHASE, BLK),
        check_vma=False,
    )
```

```python
import jax
import jax.numpy as jnp
import numpy as np
from jax import lax
from jax.experimental import pallas as pl
from jax.experimental.pallas import tpu as pltpu
from jax.sharding import Mesh, PartitionSpec as P

FEAT = 8192
EPS = 1e-05
LANES = 128
PAD = 16

AXES = ("y", "xh", "xl", "zh", "zm", "z0", "core")
SIZES = (4, 2, 2, 4, 2, 2, 2)
PHASE = ("y", "xh")
BLK = ("xl", "zh", "zm", "z0", "core")
FAR = "zh"
BLOCK = ("xl", "zm", "z0")

f32, bf16 = jnp.float32, jnp.bfloat16


def exchange(value, axes):
    return lax.all_to_all(value, axes, 0, 0, tiled=True)


def route(move):
    pairs = []
    for at in np.ndindex(*SIZES):
        to = dict(zip(AXES, at))
        move(to)
        to = tuple(to[a] % n for a, n in zip(AXES, SIZES))
        pairs.append([int(np.ravel_multi_index(i, SIZES)) for i in (at, to)])
    return pairs


def send(value, move):
    return lax.ppermute(value, AXES, route(move))


def spread(turn, cross):
    def move(to):
        part, group = to["y"] * 2 + to["xh"], to["zh"] * 2 + to["zm"]
        to["y"], to["xh"] = divmod(group, 2)
        to["zh"], to["zm"] = divmod((part + turn - group) % 8, 2)
        to["core"] += cross

    return move


def shift(**by):
    def move(to):
        for axis, count in by.items():
            to[axis] += count

    return move


def cut_kernel(gate, up, out):
    zero = jnp.zeros((56 - gate.shape[0], 512), f32)
    for group in range(4):
        columns = slice(group * 512, group * 512 + 512)
        parts = (gate[:, columns].astype(f32), zero, up[:, columns].astype(f32), zero)
        out[group] = jnp.concatenate(parts).astype(bf16)


def cut(gate, up):
    units = gate.shape[0]
    return pl.pallas_call(
        cut_kernel,
        grid=(4,),
        out_shape=jax.ShapeDtypeStruct((8, 112, 1024), bf16),
        in_specs=[pl.BlockSpec((units, 2048), lambda i: (0, i))] * 2,
        out_specs=pl.BlockSpec((4, 112, 512), lambda i: (i % 2, 0, i // 2)),
        compiler_params=pltpu.CompilerParams(vmem_limit_bytes=60 * 2**20),
        cost_estimate=pl.CostEstimate(flops=0, bytes_accessed=8 * units * FEAT, transcendentals=0),
    )(gate, up)


def sums_kernel(at, x0, x1, x2, x3, w_own, w_other, out, scaled):
    rows = scaled.shape[0]
    squares = jnp.zeros((rows, LANES), f32)
    for chip, block in enumerate((x0, x1, x2, x3)):
        for core in (0, 1):
            vals = block[core, :rows].astype(f32)
            gain = block[core, rows:].astype(f32)[:1]
            squares += vals * vals
            place = (jnp.bitwise_xor(at[1], chip) * 2 + jnp.bitwise_xor(at[0], core)) * LANES
            scaled[:, pl.ds(pl.multiple_of(place, LANES), LANES)] = (vals * gain).astype(bf16)
    total = lax.dot_general(
        jnp.ones((8, LANES), f32),
        squares,
        (((1,), (1,)), ((), ())),
        precision=lax.Precision.HIGHEST,
        preferred_element_type=f32,
    )
    hi = total.astype(bf16).astype(f32)
    mid = (total - hi).astype(bf16).astype(f32)
    row = lax.broadcasted_iota(jnp.int32, (8, rows), 0)
    extra = jnp.where(row == 4, hi, jnp.where(row == 5, mid, jnp.where(row == 6, total - hi - mid, 0.0)))
    extra = jnp.concatenate((jnp.zeros((48, rows), f32), extra, jnp.zeros((56, rows), f32)))
    right = scaled[...]
    for side, weight in enumerate((w_own, w_other)):
        part = lax.dot_general(
            weight[...].reshape(8 * 112, 1024),
            right,
            (((1,), (1,)), ((), ())),
            preferred_element_type=f32,
        ).reshape(8, 112, rows)
        if side == 0:
            part = part + extra[None]
        out[:, side] = part.astype(bf16)


def acts_kernel(at, sums, out):
    rows = sums.shape[-1]
    own = sums[0, 0].astype(f32)
    other = sums[0, 1].astype(f32)
    for part in range(1, 8):
        own += sums[part, 0].astype(f32)
        other += sums[part, 1].astype(f32)
    row = lax.broadcasted_iota(jnp.int32, (8, rows), 0)
    squares = jnp.where((row >= 4) & (row < 7), own[48:56], 0.0)
    inv_rms = lax.rsqrt(jnp.sum(squares, 0, keepdims=True) / FEAT + EPS)
    acts = []
    for total in (own, other):
        gate = total[:52] * inv_rms
        acts.append(gate / (1.0 + jnp.exp(-gate)) * (total[56:108] * inv_rms))
    swapped = at[0] == 1
    acts = (jnp.where(swapped, acts[1], acts[0]), jnp.where(swapped, acts[0], acts[1]))
    acts = jnp.concatenate(acts).astype(bf16)
    for copy in range(4):
        out[copy] = acts


def place_kernel(at, parts, out):
    total = parts[0].astype(f32)
    for part in range(1, 8):
        total += parts[part].astype(f32)
    for piece in range(16):
        column = piece * LANES
        out[jnp.bitwise_xor(at[2], piece)] = total[:, column : column + LANES].astype(bf16)


def run(kernel, out_shape, operands, scratch=(), flops=0, vmem=32):
    moved = sum(o.size * o.dtype.itemsize for o in operands) + int(np.prod(out_shape)) * 2
    return pl.pallas_call(
        kernel,
        out_shape=jax.ShapeDtypeStruct(out_shape, bf16),
        in_specs=[pl.BlockSpec(memory_space=pltpu.SMEM)]
        + [pl.BlockSpec(memory_space=pltpu.VMEM)] * (len(operands) - 1),
        out_specs=pl.BlockSpec(memory_space=pltpu.VMEM),
        scratch_shapes=list(scratch),
        compiler_params=pltpu.CompilerParams(vmem_limit_bytes=vmem * 2**20),
        cost_estimate=pl.CostEstimate(flops=flops, bytes_accessed=moved, transcendentals=0),
    )(*operands)


def local(layer_input, norm_gain, gate_weight, up_weight, down_weight):
    phase, core = lax.axis_index(PHASE), lax.axis_index("core")
    at = (core, lax.axis_index(("xl", "z0")), lax.axis_index((*BLOCK, "core")))
    at = jnp.stack(at).astype(jnp.int32)
    units = gate_weight.shape[0]
    rows = layer_input.shape[0] // 2

    halves = layer_input.reshape(8, 2, rows // 8, LANES)
    gain = jnp.broadcast_to(norm_gain[None], (PAD, LANES))

    def half(index):
        part = lax.dynamic_slice_in_dim(halves, index, 1, 1).reshape(rows, LANES)
        return jnp.concatenate((part, gain))

    def halve(value, axis):
        place = lax.axis_index(axis)
        kept, sent = (
            lax.dynamic_index_in_dim(value, i, 0, keepdims=False) for i in (place, 1 - place)
        )
        return kept, send(sent, shift(**{axis: 1}))

    down = down_weight.reshape(2, 4, 2, 2, 2 * units, LANES)
    down = down.transpose(3, 2, 0, 1, 4, 5).reshape(2, 2, 2, 8 * units, LANES)
    down = jnp.stack(halve(down, "z0"), 2)

    own_w = exchange(cut(gate_weight, up_weight), PHASE)
    first = send(half(core), spread(0, 0))
    second = send(half(1 - core), spread(4, 1))
    first, second, own_w, down = lax.optimization_barrier((first, second, own_w, down))
    other_w = send(own_w, shift(core=1))
    held = jnp.stack((first, second))
    blocks = [held] + [send(held, shift(xl=i, z0=j)) for i, j in ((0, 1), (1, 0), (1, 1))]

    sums = run(
        sums_kernel,
        (8, 2, 112, rows),
        (at, *blocks, own_w, other_w),
        (pltpu.VMEM((rows, 1024), bf16),),
        flops=2 * 1792 * 1024 * rows,
        vmem=40,
    )
    zm, xl = lax.axis_index("zm"), lax.axis_index("xl")

    def piece(xl_off, zm_off):
        part = lax.dynamic_index_in_dim(down, jnp.bitwise_xor(zm, zm_off), 0, keepdims=False)
        part = lax.dynamic_index_in_dim(part, jnp.bitwise_xor(xl, xl_off), 0, keepdims=False)
        return send(part, shift(xl=xl_off, zm=zm_off)) if xl_off or zm_off else part

    pieces = [piece(xl_off, zm_off) for xl_off in (0, 1) for zm_off in (0, 1)]
    acts = run(acts_kernel, (4, 2 * units, rows), (at, exchange(sums, PHASE)))
    acts, *pieces = lax.optimization_barrier((acts, *pieces))
    down = jnp.stack(pieces).reshape(8, 8 * units, LANES)
    down = jnp.stack((down, send(down, shift(core=1))), 1)
    down = down.transpose(2, 0, 1, 3).reshape(8 * units, 2048)
    acts = exchange(acts, FAR).reshape(8 * units, rows)
    partials = lax.dot_general(
        acts, down, (((0,), (0,)), ((), ())), preferred_element_type=f32
    ).astype(bf16)
    partials = exchange(partials.reshape(8, rows // 8, 2048), PHASE)
    partials = run(place_kernel, (16, rows // 8, LANES), (at, partials))
    partials = exchange(partials, (*BLOCK, "core")).astype(f32)
    ffn_out = jnp.sum(partials.reshape(8, rows // 4, LANES), 0)
    residual = lax.dynamic_slice_in_dim(layer_input, phase * (rows // 4), rows // 4, 0)
    return (residual.astype(f32) + ffn_out).astype(bf16)


def solution(mesh):
    fine = Mesh(mesh.devices.reshape(SIZES), AXES)
    return jax.shard_map(
        local,
        mesh=fine,
        in_specs=(
            P(None, BLK),
            P(BLK),
            P((*PHASE, *BLK), None),
            P((*PHASE, *BLK), None),
            P(PHASE, BLK),
        ),
        out_specs=P(PHASE, BLK),
        check_vma=False,
    )
```

```python
import jax
import jax.numpy as jnp
import numpy as np
from jax import lax
from jax.experimental import pallas as pl
from jax.experimental.pallas import tpu as pltpu
from jax.sharding import Mesh, PartitionSpec as P

FEAT = 8192
EPS = 1e-05
LANES = 128
PAD = 16

AXES = ("y", "xh", "xl", "zh", "zm", "z0", "core")
SIZES = (4, 2, 2, 4, 2, 2, 2)
PHASE = ("y", "xh")
BLK = ("xl", "zh", "zm", "z0", "core")
FAR = "zh"
BLOCK = ("xl", "zm", "z0")

f32, bf16 = jnp.float32, jnp.bfloat16


def exchange(value, axes):
    return lax.all_to_all(value, axes, 0, 0, tiled=True)


def route(move):
    pairs = []
    for at in np.ndindex(*SIZES):
        to = dict(zip(AXES, at))
        move(to)
        to = tuple(to[a] % n for a, n in zip(AXES, SIZES))
        pairs.append([int(np.ravel_multi_index(i, SIZES)) for i in (at, to)])
    return pairs


def send(value, move):
    return lax.ppermute(value, AXES, route(move))


def spread(turn, cross):
    def move(to):
        part, group = to["y"] * 2 + to["xh"], to["zh"] * 2 + to["zm"]
        to["y"], to["xh"] = divmod(group, 2)
        to["zh"], to["zm"] = divmod((part + turn - group) % 8, 2)
        to["core"] += cross

    return move


def shift(**by):
    def move(to):
        for axis, count in by.items():
            to[axis] += count

    return move


def cut_kernel(gate, up, out):
    zero = jnp.zeros((56 - gate.shape[0], 512), f32)
    for group in range(4):
        columns = slice(group * 512, group * 512 + 512)
        parts = (gate[:, columns].astype(f32), zero, up[:, columns].astype(f32), zero)
        out[group] = jnp.concatenate(parts).astype(bf16)


def cut(gate, up):
    units = gate.shape[0]
    return pl.pallas_call(
        cut_kernel,
        grid=(4,),
        out_shape=jax.ShapeDtypeStruct((8, 112, 1024), bf16),
        in_specs=[pl.BlockSpec((units, 2048), lambda i: (0, i))] * 2,
        out_specs=pl.BlockSpec((4, 112, 512), lambda i: (i % 2, 0, i // 2)),
        compiler_params=pltpu.CompilerParams(vmem_limit_bytes=60 * 2**20),
        cost_estimate=pl.CostEstimate(flops=0, bytes_accessed=8 * units * FEAT, transcendentals=0),
    )(gate, up)


def sums_kernel(at, x0, x1, x2, x3, w_own, w_other, out, scaled):
    rows = scaled.shape[0]
    squares = jnp.zeros((rows, LANES), f32)
    for chip, block in enumerate((x0, x1, x2, x3)):
        for core in (0, 1):
            vals = block[core, :rows].astype(f32)
            gain = block[core, rows:].astype(f32)[:1]
            squares += vals * vals
            place = (jnp.bitwise_xor(at[1], chip) * 2 + jnp.bitwise_xor(at[0], core)) * LANES
            scaled[:, pl.ds(pl.multiple_of(place, LANES), LANES)] = (vals * gain).astype(bf16)
    total = lax.dot_general(
        jnp.ones((8, LANES), f32),
        squares,
        (((1,), (1,)), ((), ())),
        precision=lax.Precision.HIGHEST,
        preferred_element_type=f32,
    )
    hi = total.astype(bf16).astype(f32)
    mid = (total - hi).astype(bf16).astype(f32)
    row = lax.broadcasted_iota(jnp.int32, (8, rows), 0)
    extra = jnp.where(row == 4, hi, jnp.where(row == 5, mid, jnp.where(row == 6, total - hi - mid, 0.0)))
    extra = jnp.concatenate((jnp.zeros((48, rows), f32), extra, jnp.zeros((56, rows), f32)))
    right = scaled[...]
    for side, weight in enumerate((w_own, w_other)):
        part = lax.dot_general(
            weight[...].reshape(8 * 112, 1024),
            right,
            (((1,), (1,)), ((), ())),
            preferred_element_type=f32,
        ).reshape(8, 112, rows)
        if side == 0:
            part = part + extra[None]
        out[:, side] = part.astype(bf16)


def acts_kernel(at, sums, out):
    rows = sums.shape[-1]
    own = sums[0, 0].astype(f32)
    other = sums[0, 1].astype(f32)
    for part in range(1, 8):
        own += sums[part, 0].astype(f32)
        other += sums[part, 1].astype(f32)
    row = lax.broadcasted_iota(jnp.int32, (8, rows), 0)
    squares = jnp.where((row >= 4) & (row < 7), own[48:56], 0.0)
    inv_rms = lax.rsqrt(jnp.sum(squares, 0, keepdims=True) / FEAT + EPS)
    acts = []
    for total in (own, other):
        gate = total[:52] * inv_rms
        acts.append(gate / (1.0 + jnp.exp(-gate)) * (total[56:108] * inv_rms))
    swapped = at[0] == 1
    acts = (jnp.where(swapped, acts[1], acts[0]), jnp.where(swapped, acts[0], acts[1]))
    acts = jnp.concatenate(acts).astype(bf16)
    for copy in range(4):
        out[copy] = acts


def place_kernel(at, parts, out):
    total = parts[0].astype(f32)
    for part in range(1, 8):
        total += parts[part].astype(f32)
    for piece in range(16):
        column = piece * LANES
        out[jnp.bitwise_xor(at[2], piece)] = total[:, column : column + LANES].astype(bf16)


def run(kernel, out_shape, operands, scratch=(), flops=0, vmem=32):
    moved = sum(o.size * o.dtype.itemsize for o in operands) + int(np.prod(out_shape)) * 2
    return pl.pallas_call(
        kernel,
        out_shape=jax.ShapeDtypeStruct(out_shape, bf16),
        in_specs=[pl.BlockSpec(memory_space=pltpu.SMEM)]
        + [pl.BlockSpec(memory_space=pltpu.VMEM)] * (len(operands) - 1),
        out_specs=pl.BlockSpec(memory_space=pltpu.VMEM),
        scratch_shapes=list(scratch),
        compiler_params=pltpu.CompilerParams(vmem_limit_bytes=vmem * 2**20),
        cost_estimate=pl.CostEstimate(flops=flops, bytes_accessed=moved, transcendentals=0),
    )(*operands)


def local(layer_input, norm_gain, gate_weight, up_weight, down_weight):
    phase, core = lax.axis_index(PHASE), lax.axis_index("core")
    at = (core, lax.axis_index(("xl", "z0")), lax.axis_index((*BLOCK, "core")))
    at = jnp.stack(at).astype(jnp.int32)
    units = gate_weight.shape[0]
    rows = layer_input.shape[0] // 2

    halves = layer_input.reshape(8, 2, rows // 8, LANES)
    gain = jnp.broadcast_to(norm_gain[None], (PAD, LANES))

    def half(index):
        part = lax.dynamic_slice_in_dim(halves, index, 1, 1).reshape(rows, LANES)
        return jnp.concatenate((part, gain))

    def halve(value, axis):
        place = lax.axis_index(axis)
        kept, sent = (
            lax.dynamic_index_in_dim(value, i, 0, keepdims=False) for i in (place, 1 - place)
        )
        return kept, send(sent, shift(**{axis: 1}))

    down = down_weight.reshape(2, 4, 2, 2, 2 * units, LANES)
    down = down.transpose(3, 2, 0, 1, 4, 5).reshape(2, 2, 2, 8 * units, LANES)
    down = jnp.stack(halve(down, "z0"), 2)

    own_w = exchange(cut(gate_weight, up_weight), PHASE)
    first = send(half(core), spread(0, 0))
    second = send(half(1 - core), spread(4, 1))
    first, second, own_w, down = lax.optimization_barrier((first, second, own_w, down))
    other_w = send(own_w, shift(core=1))
    held = jnp.stack((first, second))
    blocks = [held] + [send(held, shift(xl=i, z0=j)) for i, j in ((0, 1), (1, 0), (1, 1))]

    sums = run(
        sums_kernel,
        (8, 2, 112, rows),
        (at, *blocks, own_w, other_w),
        (pltpu.VMEM((rows, 1024), bf16),),
        flops=2 * 1792 * 1024 * rows,
        vmem=40,
    )
    zm, xl = lax.axis_index("zm"), lax.axis_index("xl")

    def piece(xl_off, zm_off):
        part = lax.dynamic_index_in_dim(down, jnp.bitwise_xor(zm, zm_off), 0, keepdims=False)
        return lax.dynamic_index_in_dim(part, jnp.bitwise_xor(xl, xl_off), 0, keepdims=False)

    onward = send(piece(1, 1), shift(zm=1))
    across = send(piece(0, 1), shift(zm=1))
    sums, onward = lax.optimization_barrier((exchange(sums, PHASE), onward))
    acts = run(acts_kernel, (4, 2 * units, rows), (at, sums))
    acts, across = lax.optimization_barrier((acts, across))
    pieces = (piece(0, 0), across, send(piece(1, 0), shift(xl=1)), send(onward, shift(xl=1)))
    down = jnp.stack(pieces).reshape(8, 8 * units, LANES)
    down = jnp.stack((down, send(down, shift(core=1))), 1)
    down = down.transpose(2, 0, 1, 3).reshape(8 * units, 2048)
    acts = exchange(acts, FAR).reshape(8 * units, rows)
    partials = lax.dot_general(
        acts, down, (((0,), (0,)), ((), ())), preferred_element_type=f32
    ).astype(bf16)
    partials = exchange(partials.reshape(8, rows // 8, 2048), PHASE)
    partials = run(place_kernel, (16, rows // 8, LANES), (at, partials))
    partials = exchange(partials, (*BLOCK, "core")).astype(f32)
    ffn_out = jnp.sum(partials.reshape(8, rows // 4, LANES), 0)
    residual = lax.dynamic_slice_in_dim(layer_input, phase * (rows // 4), rows // 4, 0)
    return (residual.astype(f32) + ffn_out).astype(bf16)


def solution(mesh):
    fine = Mesh(mesh.devices.reshape(SIZES), AXES)
    return jax.shard_map(
        local,
        mesh=fine,
        in_specs=(
            P(None, BLK),
            P(BLK),
            P((*PHASE, *BLK), None),
            P((*PHASE, *BLK), None),
            P(PHASE, BLK),
        ),
        out_specs=P(PHASE, BLK),
        check_vma=False,
    )
```

```python
import jax
import jax.numpy as jnp
import numpy as np
from jax import lax
from jax.experimental import pallas as pl
from jax.experimental.pallas import tpu as pltpu
from jax.sharding import Mesh, PartitionSpec as P

FEAT = 8192
EPS = 1e-05
LANES = 128
PAD = 16

AXES = ("y", "xh", "xl", "zh", "zm", "z0", "core")
SIZES = (4, 2, 2, 4, 2, 2, 2)
PHASE = ("y", "xh")
BLK = ("xl", "zh", "zm", "z0", "core")
FAR = "zh"
BLOCK = ("xl", "zm", "z0")

f32, bf16 = jnp.float32, jnp.bfloat16


def exchange(value, axes):
    return lax.all_to_all(value, axes, 0, 0, tiled=True)


def route(move):
    pairs = []
    for at in np.ndindex(*SIZES):
        to = dict(zip(AXES, at))
        move(to)
        to = tuple(to[a] % n for a, n in zip(AXES, SIZES))
        pairs.append([int(np.ravel_multi_index(i, SIZES)) for i in (at, to)])
    return pairs


def send(value, move):
    return lax.ppermute(value, AXES, route(move))


def spread(turn, cross):
    def move(to):
        part, group = to["y"] * 2 + to["xh"], to["zh"] * 2 + to["zm"]
        to["y"], to["xh"] = divmod(group, 2)
        to["zh"], to["zm"] = divmod((part + turn - group) % 8, 2)
        to["core"] += cross

    return move


def shift(**by):
    def move(to):
        for axis, count in by.items():
            to[axis] += count

    return move


def cut_kernel(gate, up, out):
    zero = jnp.zeros((56 - gate.shape[0], 512), f32)
    for group in range(8):
        columns = slice(group * 512, group * 512 + 512)
        parts = (gate[:, columns].astype(f32), zero, up[:, columns].astype(f32), zero)
        out[group] = jnp.concatenate(parts).astype(bf16)


def cut(gate, up):
    units = gate.shape[0]
    return pl.pallas_call(
        cut_kernel,
        grid=(2,),
        out_shape=jax.ShapeDtypeStruct((8, 112, 1024), bf16),
        in_specs=[pl.BlockSpec((units, 4096), lambda i: (0, i))] * 2,
        out_specs=pl.BlockSpec((8, 112, 512), lambda i: (0, 0, i)),
        compiler_params=pltpu.CompilerParams(vmem_limit_bytes=60 * 2**20),
        cost_estimate=pl.CostEstimate(flops=0, bytes_accessed=8 * units * FEAT, transcendentals=0),
    )(gate, up)


def sums_kernel(at, x0, x1, x2, x3, w_own, w_other, out, scaled):
    rows = scaled.shape[0]
    squares = jnp.zeros((rows, LANES), f32)
    for chip, block in enumerate((x0, x1, x2, x3)):
        for core in (0, 1):
            vals = block[core, :rows].astype(f32)
            gain = block[core, rows:].astype(f32)[:1]
            squares += vals * vals
            place = (jnp.bitwise_xor(at[1], chip) * 2 + jnp.bitwise_xor(at[0], core)) * LANES
            scaled[:, pl.ds(pl.multiple_of(place, LANES), LANES)] = (vals * gain).astype(bf16)
    total = lax.dot_general(
        jnp.ones((8, LANES), f32),
        squares,
        (((1,), (1,)), ((), ())),
        precision=lax.Precision.HIGHEST,
        preferred_element_type=f32,
    )
    hi = total.astype(bf16).astype(f32)
    mid = (total - hi).astype(bf16).astype(f32)
    row = lax.broadcasted_iota(jnp.int32, (8, rows), 0)
    extra = jnp.where(row == 4, hi, jnp.where(row == 5, mid, jnp.where(row == 6, total - hi - mid, 0.0)))
    extra = jnp.concatenate((jnp.zeros((48, rows), f32), extra, jnp.zeros((56, rows), f32)))
    right = scaled[...]
    for side, weight in enumerate((w_own, w_other)):
        part = lax.dot_general(
            weight[...].reshape(8 * 112, 1024),
            right,
            (((1,), (1,)), ((), ())),
            preferred_element_type=f32,
        ).reshape(8, 112, rows)
        if side == 0:
            part = part + extra[None]
        out[:, side] = part.astype(bf16)


def acts_kernel(at, sums, out):
    rows = sums.shape[-1]
    own = sums[0, 0].astype(f32)
    other = sums[0, 1].astype(f32)
    for part in range(1, 8):
        own += sums[part, 0].astype(f32)
        other += sums[part, 1].astype(f32)
    row = lax.broadcasted_iota(jnp.int32, (8, rows), 0)
    squares = jnp.where((row >= 4) & (row < 7), own[48:56], 0.0)
    inv_rms = lax.rsqrt(jnp.sum(squares, 0, keepdims=True) / FEAT + EPS)
    acts = []
    for total in (own, other):
        gate = total[:52] * inv_rms
        acts.append(gate / (1.0 + jnp.exp(-gate)) * (total[56:108] * inv_rms))
    swapped = at[0] == 1
    acts = (jnp.where(swapped, acts[1], acts[0]), jnp.where(swapped, acts[0], acts[1]))
    acts = jnp.concatenate(acts).astype(bf16)
    for copy in range(4):
        out[copy] = acts


def place_kernel(at, parts, out):
    total = parts[0].astype(f32)
    for part in range(1, 8):
        total += parts[part].astype(f32)
    for piece in range(16):
        column = piece * LANES
        out[jnp.bitwise_xor(at[2], piece)] = total[:, column : column + LANES].astype(bf16)


def run(kernel, out_shape, operands, scratch=(), flops=0, vmem=32):
    moved = sum(o.size * o.dtype.itemsize for o in operands) + int(np.prod(out_shape)) * 2
    return pl.pallas_call(
        kernel,
        out_shape=jax.ShapeDtypeStruct(out_shape, bf16),
        in_specs=[pl.BlockSpec(memory_space=pltpu.SMEM)]
        + [pl.BlockSpec(memory_space=pltpu.VMEM)] * (len(operands) - 1),
        out_specs=pl.BlockSpec(memory_space=pltpu.VMEM),
        scratch_shapes=list(scratch),
        compiler_params=pltpu.CompilerParams(vmem_limit_bytes=vmem * 2**20),
        cost_estimate=pl.CostEstimate(flops=flops, bytes_accessed=moved, transcendentals=0),
    )(*operands)


def local(layer_input, norm_gain, gate_weight, up_weight, down_weight):
    phase, core = lax.axis_index(PHASE), lax.axis_index("core")
    at = (core, lax.axis_index(("xl", "z0")), lax.axis_index((*BLOCK, "core")))
    at = jnp.stack(at).astype(jnp.int32)
    units = gate_weight.shape[0]
    rows = layer_input.shape[0] // 2

    halves = layer_input.reshape(8, 2, rows // 8, LANES)
    gain = jnp.broadcast_to(norm_gain[None], (PAD, LANES))

    def half(index):
        part = lax.dynamic_slice_in_dim(halves, index, 1, 1).reshape(rows, LANES)
        return jnp.concatenate((part, gain))

    down = down_weight.reshape(2, 4, 2, 2, 2 * units, LANES)
    down = down.transpose(3, 2, 0, 1, 4, 5).reshape(2, 2, 2, 8 * units, LANES)
    z0 = lax.axis_index("z0")
    kept, sent = (lax.dynamic_index_in_dim(down, i, 0, keepdims=False) for i in (z0, 1 - z0))
    got = send(sent, shift(z0=1))

    own_w = exchange(cut(gate_weight, up_weight), PHASE)
    first = send(half(core), spread(0, 0))
    second = send(half(1 - core), spread(4, 1))
    held, own_w, kept, got = lax.optimization_barrier((jnp.stack((first, second)), own_w, kept, got))
    other_w = send(own_w, shift(core=1))
    down = jnp.stack((kept, got), 2)
    blocks = [held] + [send(held, shift(xl=i, z0=j)) for i, j in ((0, 1), (1, 0), (1, 1))]

    sums = run(
        sums_kernel,
        (8, 2, 112, rows),
        (at, *blocks, own_w, other_w),
        (pltpu.VMEM((rows, 1024), bf16),),
        flops=2 * 1792 * 1024 * rows,
        vmem=40,
    )
    zm, xl = lax.axis_index("zm"), lax.axis_index("xl")

    def piece(xl_off, zm_off):
        part = lax.dynamic_index_in_dim(down, jnp.bitwise_xor(zm, zm_off), 0, keepdims=False)
        return lax.dynamic_index_in_dim(part, jnp.bitwise_xor(xl, xl_off), 0, keepdims=False)

    onward = send(piece(1, 1), shift(zm=1))
    across = send(piece(0, 1), shift(zm=1))
    sums, onward = lax.optimization_barrier((exchange(sums, PHASE), onward))
    acts = run(acts_kernel, (4, 2 * units, rows), (at, sums))
    acts, across = lax.optimization_barrier((acts, across))
    pieces = (piece(0, 0), across, send(piece(1, 0), shift(xl=1)), send(onward, shift(xl=1)))
    down = jnp.stack(pieces).reshape(8, 8 * units, LANES)
    down = jnp.stack((down, send(down, shift(core=1))), 1)
    down = down.transpose(2, 0, 1, 3).reshape(8 * units, 2048)
    acts = exchange(acts, FAR).reshape(8 * units, rows)
    partials = lax.dot_general(
        acts, down, (((0,), (0,)), ((), ())), preferred_element_type=f32
    ).astype(bf16)
    partials = exchange(partials.reshape(8, rows // 8, 2048), PHASE)
    partials = run(place_kernel, (16, rows // 8, LANES), (at, partials))
    partials = exchange(partials, (*BLOCK, "core")).astype(f32)
    ffn_out = jnp.sum(partials.reshape(8, rows // 4, LANES), 0)
    residual = lax.dynamic_slice_in_dim(layer_input, phase * (rows // 4), rows // 4, 0)
    return (residual.astype(f32) + ffn_out).astype(bf16)


def solution(mesh):
    fine = Mesh(mesh.devices.reshape(SIZES), AXES)
    return jax.shard_map(
        local,
        mesh=fine,
        in_specs=(
            P(None, BLK),
            P(BLK),
            P((*PHASE, *BLK), None),
            P((*PHASE, *BLK), None),
            P(PHASE, BLK),
        ),
        out_specs=P(PHASE, BLK),
        check_vma=False,
    )
```

```python
import jax
import jax.numpy as jnp
import numpy as np
from jax import lax
from jax.experimental import pallas as pl
from jax.experimental.pallas import tpu as pltpu
from jax.sharding import Mesh, PartitionSpec as P

FEAT = 8192
EPS = 1e-05
LANES = 128
PAD = 16

AXES = ("y", "xh", "xl", "zh", "zm", "z0", "core")
SIZES = (4, 2, 2, 4, 2, 2, 2)
PHASE = ("y", "xh")
BLK = ("xl", "zh", "zm", "z0", "core")
FAR = "zh"
BLOCK = ("xl", "zm", "z0")

f32, bf16 = jnp.float32, jnp.bfloat16


def exchange(value, axes):
    return lax.all_to_all(value, axes, 0, 0, tiled=True)


def route(move):
    pairs = []
    for at in np.ndindex(*SIZES):
        to = dict(zip(AXES, at))
        move(to)
        to = tuple(to[a] % n for a, n in zip(AXES, SIZES))
        pairs.append([int(np.ravel_multi_index(i, SIZES)) for i in (at, to)])
    return pairs


def send(value, move):
    return lax.ppermute(value, AXES, route(move))


def spread(turn, cross):
    def move(to):
        part, group = to["y"] * 2 + to["xh"], to["zh"] * 2 + to["zm"]
        to["y"], to["xh"] = divmod(group, 2)
        to["zh"], to["zm"] = divmod((part + turn - group) % 8, 2)
        to["core"] += cross

    return move


def shift(**by):
    def move(to):
        for axis, count in by.items():
            to[axis] += count

    return move


def cut_kernel(gate, up, out):
    zero = jnp.zeros((56 - gate.shape[0], 512), f32)
    for group in range(8):
        columns = slice(group * 512, group * 512 + 512)
        parts = (gate[:, columns].astype(f32), zero, up[:, columns].astype(f32), zero)
        out[group] = jnp.concatenate(parts).astype(bf16)


def cut(gate, up):
    units = gate.shape[0]
    return pl.pallas_call(
        cut_kernel,
        grid=(2,),
        out_shape=jax.ShapeDtypeStruct((8, 112, 1024), bf16),
        in_specs=[pl.BlockSpec((units, 4096), lambda i: (0, i))] * 2,
        out_specs=pl.BlockSpec((8, 112, 512), lambda i: (0, 0, i)),
        compiler_params=pltpu.CompilerParams(vmem_limit_bytes=60 * 2**20),
        cost_estimate=pl.CostEstimate(flops=0, bytes_accessed=8 * units * FEAT, transcendentals=0),
    )(gate, up)


def sums_kernel(at, x0, x1, x2, x3, w_own, w_other, out, scaled):
    rows = scaled.shape[0]
    squares = jnp.zeros((rows, LANES), f32)
    for chip, block in enumerate((x0, x1, x2, x3)):
        for core in (0, 1):
            vals = block[core, :rows].astype(f32)
            gain = block[core, rows:].astype(f32)[:1]
            squares += vals * vals
            place = (jnp.bitwise_xor(at[1], chip) * 2 + jnp.bitwise_xor(at[0], core)) * LANES
            scaled[:, pl.ds(pl.multiple_of(place, LANES), LANES)] = (vals * gain).astype(bf16)
    total = lax.dot_general(
        jnp.ones((8, LANES), f32),
        squares,
        (((1,), (1,)), ((), ())),
        precision=lax.Precision.HIGHEST,
        preferred_element_type=f32,
    )
    hi = total.astype(bf16).astype(f32)
    mid = (total - hi).astype(bf16).astype(f32)
    row = lax.broadcasted_iota(jnp.int32, (8, rows), 0)
    extra = jnp.where(row == 4, hi, jnp.where(row == 5, mid, jnp.where(row == 6, total - hi - mid, 0.0)))
    extra = jnp.concatenate((jnp.zeros((48, rows), f32), extra, jnp.zeros((56, rows), f32)))
    right = scaled[...]
    for side, weight in enumerate((w_own, w_other)):
        part = lax.dot_general(
            weight[...].reshape(8 * 112, 1024),
            right,
            (((1,), (1,)), ((), ())),
            preferred_element_type=f32,
        ).reshape(8, 112, rows)
        if side == 0:
            part = part + extra[None]
        out[:, side] = part.astype(bf16)


def acts_kernel(at, sums, out):
    rows = sums.shape[-1]
    own = sums[0, 0].astype(f32)
    other = sums[0, 1].astype(f32)
    for part in range(1, 8):
        own += sums[part, 0].astype(f32)
        other += sums[part, 1].astype(f32)
    row = lax.broadcasted_iota(jnp.int32, (8, rows), 0)
    squares = jnp.where((row >= 4) & (row < 7), own[48:56], 0.0)
    inv_rms = lax.rsqrt(jnp.sum(squares, 0, keepdims=True) / FEAT + EPS)
    acts = []
    for total in (own, other):
        gate = total[:52] * inv_rms
        acts.append(gate / (1.0 + jnp.exp(-gate)) * (total[56:108] * inv_rms))
    swapped = at[0] == 1
    acts = (jnp.where(swapped, acts[1], acts[0]), jnp.where(swapped, acts[0], acts[1]))
    acts = jnp.concatenate(acts).astype(bf16)
    for copy in range(4):
        out[copy] = acts


def place_kernel(at, parts, out):
    total = parts[0].astype(f32)
    for part in range(1, 8):
        total += parts[part].astype(f32)
    for piece in range(16):
        column = piece * LANES
        out[jnp.bitwise_xor(at[2], piece)] = total[:, column : column + LANES].astype(bf16)


def run(kernel, out_shape, operands, scratch=(), flops=0, vmem=32):
    moved = sum(o.size * o.dtype.itemsize for o in operands) + int(np.prod(out_shape)) * 2
    return pl.pallas_call(
        kernel,
        out_shape=jax.ShapeDtypeStruct(out_shape, bf16),
        in_specs=[pl.BlockSpec(memory_space=pltpu.SMEM)]
        + [pl.BlockSpec(memory_space=pltpu.VMEM)] * (len(operands) - 1),
        out_specs=pl.BlockSpec(memory_space=pltpu.VMEM),
        scratch_shapes=list(scratch),
        compiler_params=pltpu.CompilerParams(vmem_limit_bytes=vmem * 2**20),
        cost_estimate=pl.CostEstimate(flops=flops, bytes_accessed=moved, transcendentals=0),
    )(*operands)


def local(layer_input, norm_gain, gate_weight, up_weight, down_weight):
    phase, core = lax.axis_index(PHASE), lax.axis_index("core")
    at = (core, lax.axis_index(("xl", "z0")), lax.axis_index((*BLOCK, "core")))
    at = jnp.stack(at).astype(jnp.int32)
    units = gate_weight.shape[0]
    rows = layer_input.shape[0] // 2

    halves = layer_input.reshape(8, 2, rows // 8, LANES)
    gain = jnp.broadcast_to(norm_gain[None], (PAD, LANES))

    def half(index):
        part = lax.dynamic_slice_in_dim(halves, index, 1, 1).reshape(rows, LANES)
        return jnp.concatenate((part, gain))

    down = down_weight.reshape(2, 4, 2, 2, 2 * units, LANES)
    down = down.transpose(3, 2, 0, 1, 4, 5).reshape(2, 2, 2, 8 * units, LANES)
    z0 = lax.axis_index("z0")
    kept, sent = (lax.dynamic_index_in_dim(down, i, 0, keepdims=False) for i in (z0, 1 - z0))
    got = send(sent, shift(z0=1))

    own_w = exchange(cut(gate_weight, up_weight), PHASE)
    first = send(half(core), spread(0, 0))
    second = send(half(1 - core), spread(4, 1))
    held, own_w, kept, got = lax.optimization_barrier((jnp.stack((first, second)), own_w, kept, got))
    other_w = send(own_w, shift(core=1))
    down = jnp.stack((kept, got), 2)
    blocks = [held] + [send(held, shift(xl=i, z0=j)) for i, j in ((0, 1), (1, 0), (1, 1))]

    sums = run(
        sums_kernel,
        (8, 2, 112, rows),
        (at, *blocks, own_w, other_w),
        (pltpu.VMEM((rows, 1024), bf16),),
        flops=2 * 1792 * 1024 * rows,
        vmem=54,
    )
    zm, xl = lax.axis_index("zm"), lax.axis_index("xl")

    def piece(xl_off, zm_off):
        part = lax.dynamic_index_in_dim(down, jnp.bitwise_xor(zm, zm_off), 0, keepdims=False)
        return lax.dynamic_index_in_dim(part, jnp.bitwise_xor(xl, xl_off), 0, keepdims=False)

    onward = send(piece(1, 1), shift(zm=1))
    across = send(piece(0, 1), shift(zm=1))
    sums, onward = lax.optimization_barrier((exchange(sums, PHASE), onward))
    acts = run(acts_kernel, (4, 2 * units, rows), (at, sums))
    acts, across = lax.optimization_barrier((acts, across))
    pieces = (piece(0, 0), across, send(piece(1, 0), shift(xl=1)), send(onward, shift(xl=1)))
    down = jnp.stack(pieces).reshape(8, 8 * units, LANES)
    down = jnp.stack((down, send(down, shift(core=1))), 1)
    down = down.transpose(2, 0, 1, 3).reshape(8 * units, 2048)
    acts = exchange(acts, FAR).reshape(8 * units, rows)
    partials = lax.dot_general(
        acts, down, (((0,), (0,)), ((), ())), preferred_element_type=f32
    ).astype(bf16)
    partials = exchange(partials.reshape(8, rows // 8, 2048), PHASE)
    partials = run(place_kernel, (16, rows // 8, LANES), (at, partials))
    partials = exchange(partials, (*BLOCK, "core")).astype(f32)
    ffn_out = jnp.sum(partials.reshape(8, rows // 4, LANES), 0)
    residual = lax.dynamic_slice_in_dim(layer_input, phase * (rows // 4), rows // 4, 0)
    return (residual.astype(f32) + ffn_out).astype(bf16)


def solution(mesh):
    fine = Mesh(mesh.devices.reshape(SIZES), AXES)
    return jax.shard_map(
        local,
        mesh=fine,
        in_specs=(
            P(None, BLK),
            P(BLK),
            P((*PHASE, *BLK), None),
            P((*PHASE, *BLK), None),
            P(PHASE, BLK),
        ),
        out_specs=P(PHASE, BLK),
        check_vma=False,
    )
```

```python
import jax
import jax.numpy as jnp
import numpy as np
from jax import lax
from jax.experimental import pallas as pl
from jax.experimental.pallas import tpu as pltpu
from jax.sharding import Mesh, PartitionSpec as P

FEAT = 8192
EPS = 1e-05
LANES = 128
PAD = 16

AXES = ("y", "xh", "xl", "zh", "zm", "z0", "core")
SIZES = (4, 2, 2, 4, 2, 2, 2)
PHASE = ("y", "xh")
BLK = ("xl", "zh", "zm", "z0", "core")
FAR = "zh"
BLOCK = ("xl", "zm", "z0")

f32, bf16 = jnp.float32, jnp.bfloat16


def exchange(value, axes):
    return lax.all_to_all(value, axes, 0, 0, tiled=True)


def route(move):
    pairs = []
    for at in np.ndindex(*SIZES):
        to = dict(zip(AXES, at))
        move(to)
        to = tuple(to[a] % n for a, n in zip(AXES, SIZES))
        pairs.append([int(np.ravel_multi_index(i, SIZES)) for i in (at, to)])
    return pairs


def send(value, move):
    return lax.ppermute(value, AXES, route(move))


def spread(turn, cross):
    def move(to):
        part, group = to["y"] * 2 + to["xh"], to["zh"] * 2 + to["zm"]
        to["y"], to["xh"] = divmod(group, 2)
        to["zh"], to["zm"] = divmod((part + turn - group) % 8, 2)
        to["core"] += cross

    return move


def shift(**by):
    def move(to):
        for axis, count in by.items():
            to[axis] += count

    return move


def cut_kernel(gate, up, out):
    zero = jnp.zeros((56 - gate.shape[0], 512), f32)
    for group in range(8):
        columns = slice(group * 512, group * 512 + 512)
        parts = (gate[:, columns].astype(f32), zero, up[:, columns].astype(f32), zero)
        out[group] = jnp.concatenate(parts).astype(bf16)


def cut(gate, up):
    units = gate.shape[0]
    return pl.pallas_call(
        cut_kernel,
        grid=(2,),
        out_shape=jax.ShapeDtypeStruct((8, 112, 1024), bf16),
        in_specs=[pl.BlockSpec((units, 4096), lambda i: (0, i))] * 2,
        out_specs=pl.BlockSpec((8, 112, 512), lambda i: (0, 0, i)),
        compiler_params=pltpu.CompilerParams(vmem_limit_bytes=60 * 2**20),
        cost_estimate=pl.CostEstimate(flops=0, bytes_accessed=8 * units * FEAT, transcendentals=0),
    )(gate, up)


def sums_kernel(at, x0, x1, x2, x3, w_own, w_other, out, scaled):
    rows = scaled.shape[0]
    squares = jnp.zeros((rows, LANES), f32)
    for chip, block in enumerate((x0, x1, x2, x3)):
        for core in (0, 1):
            vals = block[core, :rows].astype(f32)
            gain = block[core, rows:].astype(f32)[:1]
            squares += vals * vals
            place = (jnp.bitwise_xor(at[1], chip) * 2 + jnp.bitwise_xor(at[0], core)) * LANES
            scaled[:, pl.ds(pl.multiple_of(place, LANES), LANES)] = (vals * gain).astype(bf16)
    total = lax.dot_general(
        jnp.ones((8, LANES), f32),
        squares,
        (((1,), (1,)), ((), ())),
        precision=lax.Precision.HIGHEST,
        preferred_element_type=f32,
    )
    hi = total.astype(bf16).astype(f32)
    mid = (total - hi).astype(bf16).astype(f32)
    row = lax.broadcasted_iota(jnp.int32, (8, rows), 0)
    extra = jnp.where(row == 4, hi, jnp.where(row == 5, mid, jnp.where(row == 6, total - hi - mid, 0.0)))
    extra = jnp.concatenate((jnp.zeros((48, rows), f32), extra, jnp.zeros((56, rows), f32)))
    right = scaled[...]
    for side, weight in enumerate((w_own, w_other)):
        part = lax.dot_general(
            weight[...].reshape(8 * 112, 1024),
            right,
            (((1,), (1,)), ((), ())),
            preferred_element_type=f32,
        ).reshape(8, 112, rows)
        if side == 0:
            part = part + extra[None]
        out[:, side] = part.astype(bf16)


def acts_kernel(at, sums, out):
    rows = sums.shape[-1]
    own = sums[0, 0].astype(f32)
    other = sums[0, 1].astype(f32)
    for part in range(1, 8):
        own += sums[part, 0].astype(f32)
        other += sums[part, 1].astype(f32)
    row = lax.broadcasted_iota(jnp.int32, (8, rows), 0)
    squares = jnp.where((row >= 4) & (row < 7), own[48:56], 0.0)
    inv_rms = lax.rsqrt(jnp.sum(squares, 0, keepdims=True) / FEAT + EPS)
    acts = []
    for total in (own, other):
        gate = total[:52] * inv_rms
        acts.append(gate / (1.0 + jnp.exp(-gate)) * (total[56:108] * inv_rms))
    swapped = at[0] == 1
    acts = (jnp.where(swapped, acts[1], acts[0]), jnp.where(swapped, acts[0], acts[1]))
    acts = jnp.concatenate(acts).astype(bf16)
    for copy in range(4):
        out[copy] = acts


def place_kernel(at, parts, out):
    total = parts[0].astype(f32)
    for part in range(1, 8):
        total += parts[part].astype(f32)
    for piece in range(16):
        column = piece * LANES
        out[jnp.bitwise_xor(at[2], piece)] = total[:, column : column + LANES].astype(bf16)


def run(kernel, out_shape, operands, scratch=(), flops=0, vmem=32):
    moved = sum(o.size * o.dtype.itemsize for o in operands) + int(np.prod(out_shape)) * 2
    return pl.pallas_call(
        kernel,
        out_shape=jax.ShapeDtypeStruct(out_shape, bf16),
        in_specs=[pl.BlockSpec(memory_space=pltpu.SMEM)]
        + [pl.BlockSpec(memory_space=pltpu.VMEM)] * (len(operands) - 1),
        out_specs=pl.BlockSpec(memory_space=pltpu.VMEM),
        scratch_shapes=list(scratch),
        compiler_params=pltpu.CompilerParams(vmem_limit_bytes=vmem * 2**20),
        cost_estimate=pl.CostEstimate(flops=flops, bytes_accessed=moved, transcendentals=0),
    )(*operands)


def local(layer_input, norm_gain, gate_weight, up_weight, down_weight):
    phase, core = lax.axis_index(PHASE), lax.axis_index("core")
    at = (core, lax.axis_index(("xl", "z0")), lax.axis_index((*BLOCK, "core")))
    at = jnp.stack(at).astype(jnp.int32)
    units = gate_weight.shape[0]
    rows = layer_input.shape[0] // 2

    halves = layer_input.reshape(8, 2, rows // 8, LANES)
    gain = jnp.broadcast_to(norm_gain[None], (PAD, LANES))

    def half(index):
        part = lax.dynamic_slice_in_dim(halves, index, 1, 1).reshape(rows, LANES)
        return jnp.concatenate((part, gain))

    down = down_weight.reshape(2, 4, 2, 2, 2 * units, LANES)
    down = down.transpose(3, 2, 0, 1, 4, 5).reshape(2, 2, 2, 8 * units, LANES)
    z0 = lax.axis_index("z0")
    kept, sent = (lax.dynamic_index_in_dim(down, i, 0, keepdims=False) for i in (z0, 1 - z0))
    got = send(sent, shift(z0=1))

    own_w = exchange(cut(gate_weight, up_weight), PHASE)
    first = send(half(core), spread(0, 0))
    second = send(half(1 - core), spread(4, 1))
    residual = lax.dynamic_slice_in_dim(layer_input, phase * (rows // 4), rows // 4, 0)
    held = jnp.stack((first, second))
    held, own_w, kept, got, residual = lax.optimization_barrier((held, own_w, kept, got, residual))
    other_w = send(own_w, shift(core=1))
    down = jnp.stack((kept, got), 2)
    blocks = [held] + [send(held, shift(xl=i, z0=j)) for i, j in ((0, 1), (1, 0), (1, 1))]

    sums = run(
        sums_kernel,
        (8, 2, 112, rows),
        (at, *blocks, own_w, other_w),
        (pltpu.VMEM((rows, 1024), bf16),),
        flops=2 * 1792 * 1024 * rows,
        vmem=40,
    )
    zm, xl = lax.axis_index("zm"), lax.axis_index("xl")

    def piece(xl_off, zm_off):
        part = lax.dynamic_index_in_dim(down, jnp.bitwise_xor(zm, zm_off), 0, keepdims=False)
        return lax.dynamic_index_in_dim(part, jnp.bitwise_xor(xl, xl_off), 0, keepdims=False)

    onward = send(piece(1, 1), shift(zm=1))
    across = send(piece(0, 1), shift(zm=1))
    sums, onward = lax.optimization_barrier((exchange(sums, PHASE), onward))
    acts = run(acts_kernel, (4, 2 * units, rows), (at, sums))
    acts, across = lax.optimization_barrier((acts, across))
    pieces = (piece(0, 0), across, send(piece(1, 0), shift(xl=1)), send(onward, shift(xl=1)))
    down = jnp.stack(pieces).reshape(8, 8 * units, LANES)
    down = jnp.stack((down, send(down, shift(core=1))), 1)
    down = down.transpose(2, 0, 1, 3).reshape(8 * units, 2048)
    acts = exchange(acts, FAR).reshape(8 * units, rows)
    partials = lax.dot_general(
        acts, down, (((0,), (0,)), ((), ())), preferred_element_type=f32
    ).astype(bf16)
    partials = exchange(partials.reshape(8, rows // 8, 2048), PHASE)
    partials = run(place_kernel, (16, rows // 8, LANES), (at, partials))
    partials = exchange(partials, (*BLOCK, "core")).astype(f32)
    ffn_out = jnp.sum(partials.reshape(8, rows // 4, LANES), 0)
    return (residual.astype(f32) + ffn_out).astype(bf16)


def solution(mesh):
    fine = Mesh(mesh.devices.reshape(SIZES), AXES)
    return jax.shard_map(
        local,
        mesh=fine,
        in_specs=(
            P(None, BLK),
            P(BLK),
            P((*PHASE, *BLK), None),
            P((*PHASE, *BLK), None),
            P(PHASE, BLK),
        ),
        out_specs=P(PHASE, BLK),
        check_vma=False,
    )
```
